512 devices in a mesh: lat: 16 (over z_hi, x, core), lon: 32 (over z_lo, y).
Axes of the slice: x: 4, y: 8, z: 8 (z_hi: 2, z_lo: 4; z = z_hi * 4 + z_lo), core: 2. Of those that a mesh axis runs over, the one named last changes fastest.
Arguments:
- warm_start: float32 [32, 512, 2048], P(None, 'lon', 'lat'), may hold values from -2 to 2
- probe_signs: int32 [32, 512, 2048], P(None, 'lon', 'lat'), may hold values from 0 to 1
- ocean_mask: int32 [512, 2048], P('lon', 'lat'), may hold values 0 or 1
- kappa_sq: float32 [512, 2048], P('lon', 'lat'), may hold values from 0.02 to 2
- scale_field: float32 [512, 2048], P('lon', 'lat'), may hold values from 0.03 to 0.3
Outputs:
- solution: float32 [32, 512, 2048], P(None, 'lon', 'lat')
- residual: float32 [32, 512, 2048], P(None, 'lon', 'lat')
- kappa_grad: float32 [512, 2048], P('lon', 'lat')
The draws below stay inside these ranges and needn't reach their ends.
Inputs may be any that keep to these rules, and one draw needn't show every extreme that they name: `probe_signs`: 1 stands for a sign of +1 and 0 for -1. `ocean_mask`: 1 marks an ocean cell, 0 a land cell.
All inputs are finite; a program needn't handle non-finite values. No bound on the sum of `ocean_mask` on one device may be relied on, other than what follows from the above.
Results may differ from the reference program's by a relative error of at most 0.0003.
Values sent between devices are 32-bit elements; how exact they have to be, the bound alone decides.
No kernel may reach another device: no remote copies, remote signals or barrier semaphores. Data moves between devices by JAX's collectives and lax.ppermute only.
A program may use at most 64 MiB of HBM per device.

```python
import math
import jax
import jax.numpy as jnp
from jax import lax

PROBES = 32
ITERS = 3
NLON = 512
NLAT = 2048


def set_ends(result, stream_key, low, high):
    spot = [jax.random.randint(jax.random.fold_in(stream_key, axis), (), 0, length) for axis, length in enumerate(result.shape)]
    main_axis = result.shape.index(max(result.shape))
    next_to = spot[:main_axis] + [(spot[main_axis] + 1) % result.shape[main_axis]] + spot[main_axis + 1:]
    return result.at[tuple(spot)].set(low).at[tuple(next_to)].set(high)


def levels(own_key, extent, shards, smallest, high):
    def one(position, blocks):
        heights = jax.random.uniform(jax.random.fold_in(jax.random.fold_in(own_key, 6), position), (blocks,), jnp.float32, smallest / len(shards), high / len(shards))
        return jnp.repeat(jnp.exp(heights), extent[position] // blocks).reshape((-1,) + (1,) * (len(extent) - position - 1))

    loudness = one(*shards[0])
    for cut in shards[1:]:
        loudness = loudness * one(*cut)
    return loudness


def centred(key, shape, scale, reach, cuts=(), kind=jnp.bfloat16):
    factor_of = levels(key, shape, cuts, -0.22, 0.18) if cuts else 1.0
    drawn = jax.random.normal(key, shape, jnp.float32) * scale * factor_of
    return jnp.minimum(jnp.maximum(drawn, -reach), reach).astype(kind)


def setup_inputs(seed: int = 0) -> dict:
    splits = jax.random.split(jax.random.key(seed), 6)
    warm_start = centred(splits[0], (PROBES, NLON, NLAT), 0.3, 2.0, ((1, 32), (2, 16)), jnp.float32)
    probe_signs = set_ends(jax.random.randint(splits[1], (PROBES, NLON, NLAT), 0, 2), jax.random.fold_in(splits[1], 1), 0, 1).astype(jnp.int32)
    ocean_mask = set_ends((jax.random.randint(splits[2], (NLON, NLAT), 0, 8) < 7).astype(jnp.int32), jax.random.fold_in(splits[2], 1), 0, 1)
    kappa_sq = jnp.clip(jnp.exp(math.log(2.0) - 4.6051702 * jax.random.uniform(splits[3], (NLON, NLAT), jnp.float32) ** levels(splits[3], (NLON, NLAT), ((0, 32), (1, 16)), -0.2, 0.2)), 0.02, 2.0)
    scale_field = jnp.clip(jnp.exp(math.log(0.3) - 2.3025852 * jax.random.uniform(splits[4], (NLON, NLAT), jnp.float32) ** levels(splits[4], (NLON, NLAT), ((0, 32), (1, 16)), -0.2, 0.2)), 0.03, 0.3)
    return dict(warm_start=warm_start, probe_signs=probe_signs, ocean_mask=ocean_mask, kappa_sq=kappa_sq, scale_field=scale_field)


top_precision = lax.Precision.HIGHEST

def apply_k(values, wet_cells, diag_term):
    masked = values * wet_cells
    beside = jnp.roll(masked, 1, axis=1) + jnp.roll(masked, -1, axis=1)
    padded = jnp.pad(masked, ((0, 0), (0, 0), (1, 1)))
    beside = beside + padded[:, :, 2:] + padded[:, :, :-2]
    return wet_cells * (diag_term * masked - beside)

def apply_q(values, wet_cells, diag_term, scale_field):
    inner = scale_field * apply_k(values, wet_cells, diag_term)
    return apply_k(inner, wet_cells, diag_term) + (1.0 - wet_cells) * values

def gram(left, right):
    return jnp.einsum('pij,qij->pq', left, right, precision=top_precision)

def combine(base, block, coeffs):
    return base + jnp.einsum('pij,pq->qij', block, coeffs, precision=top_precision)

def solve_spd(matrix, rhs_block):
    factor = jnp.linalg.cholesky(matrix)
    return jax.scipy.linalg.cho_solve((factor, True), rhs_block)

def reference(warm_start, probe_signs, ocean_mask, kappa_sq, scale_field):
    wet_cells = ocean_mask.astype(jnp.float32)
    diag_term = kappa_sq + 4.0
    probes = 2.0 * probe_signs.astype(jnp.float32) - 1.0
    solution = warm_start
    residual = probes - apply_q(solution, wet_cells, diag_term, scale_field)
    direction = residual
    norms = gram(residual, residual)
    for iteration in range(ITERS):
        image = apply_q(direction, wet_cells, diag_term, scale_field)
        curvature = gram(direction, image)
        alpha = solve_spd(curvature, norms)
        solution = combine(solution, direction, alpha)
        residual = combine(residual, image, -alpha)
        if iteration + 1 < ITERS:
            fresh = gram(residual, residual)
            beta = solve_spd(norms, fresh)
            direction = combine(residual, direction, beta)
            norms = fresh
    stacked = apply_k(jnp.concatenate([solution, probes], axis=0), wet_cells, diag_term)
    k_solution = stacked[:PROBES]
    k_probes = stacked[PROBES:]
    terms = solution * (scale_field * k_probes) + k_solution * (scale_field * probes)
    kappa_grad = wet_cells * jnp.mean(terms, axis=0)
    return (solution, residual, kappa_grad)
```

```python
import jax
import jax.numpy as jnp
from jax import lax
from jax.experimental import pallas as pl
from jax.experimental.pallas import tpu as pltpu
from jax.sharding import Mesh
from jax.sharding import PartitionSpec as P

PROBES = 32
DEPTH = 8
ROWS = 16
LANES = 128
FIELDS = 72
SHIFT = 4.0
GAIN = 0.25
PARAMS = pltpu.CompilerParams(vmem_limit_bytes=48 * 1024 * 1024)


def pack_kernel(warm, signs, mask, kappa, scale, low, high, left, right):
    wet = mask[...].astype(jnp.float32)
    diag = kappa[...] + 4.0
    scaled = scale[...]
    block = lax.broadcasted_iota(jnp.int32, (FIELDS, LANES), 1) // DEPTH
    left_edge = jnp.zeros((FIELDS, LANES), jnp.float32)
    right_edge = jnp.zeros((FIELDS, LANES), jnp.float32)
    for i in range(ROWS):
        out = low if i < DEPTH else high
        j = i % DEPTH
        out[j, 0:PROBES, :] = warm[:, i, :]
        out[j, PROBES : 2 * PROBES, :] = 2.0 * signs[:, i, :].astype(jnp.float32) - 1.0
        out[j, 2 * PROBES :, :] = jnp.concatenate(
            [wet[i : i + 1], diag[i : i + 1], scaled[i : i + 1], jnp.zeros((5, LANES), jnp.float32)], axis=0
        )
        row = out[j]
        turned = pltpu.roll(row, DEPTH * i, 1) if i else row
        left_edge = jnp.where(block == i, turned, left_edge)
        right_edge = jnp.where(block == (i - 1) % ROWS, turned, right_edge)
    left[...] = left_edge
    right[...] = right_edge


def corner_kernel(from_left, from_right, first, last):
    lane = lax.broadcasted_iota(jnp.int32, (FIELDS, LANES), 1)
    before, after = from_left[...], from_right[...]
    first[...] = jnp.where(lane < 64, after, pltpu.roll(before, 72, 1))
    last[...] = jnp.where(lane < 64, pltpu.roll(after, 64, 1), pltpu.roll(before, 8, 1))


def krylov_kernel(
    low, high, from_left, from_right, from_next, from_prev, corner_next, corner_prev,
    sums, basis, images, probe_image,
    wide, power, inner, coef,
):
    lane = lax.broadcasted_iota(jnp.int32, (FIELDS, LANES), 1)
    for r in range(ROWS + 2 * DEPTH):
        i = r - DEPTH
        if i < 0:
            wide[r, :, 0:LANES] = from_prev[r]
            pair = corner_prev[...]
            after, before = (pltpu.roll(pair, (LANES - 8 * r) % LANES, 1), pltpu.roll(pair, (56 - 8 * r) % LANES, 1))
        elif i < ROWS:
            wide[r, :, 0:LANES] = low[i] if i < DEPTH else high[i - DEPTH]
            turn = (LANES - 8 * i) % LANES
            after, before = (pltpu.roll(from_right[...], turn, 1), pltpu.roll(from_left[...], turn, 1))
        else:
            j = i - ROWS
            wide[r, :, 0:LANES] = from_next[j]
            pair = corner_next[...]
            after, before = (pltpu.roll(pair, (LANES - 8 * j) % LANES, 1), pltpu.roll(pair, (56 - 8 * j) % LANES, 1))
        wide[r, :, LANES:] = jnp.where(lane < 64, after, before)
        wet = wide[r, 64:65, :]
        coef[r, 0:1, :] = wet
        coef[r, 1:2, :] = wide[r, 65:66, :]
        coef[r, 2:3, :] = wet * wide[r, 66:67, :]
        coef[r, 3:4, :] = GAIN * wet
        coef[r, 4:5, :] = GAIN * ((1.0 - wet) - SHIFT)

    def stencil(read, r):
        here = read(r)
        around = read(r - 1) + read(r + 1)
        around = around + (pltpu.roll(here, 1, 1) + pltpu.roll(here, 2 * LANES - 1, 1))
        return coef[r, 1:2, :] * here - around

    def half_image(read, reach):
        @pl.loop(DEPTH - reach, DEPTH + ROWS + reach, unroll=2)
        def _(r):
            inner[r] = coef[r, 2:3, :] * stencil(lambda t: coef[t, 0:1, :] * read(t), r)

    def inner_row(r):
        return inner[r]

    def warm_row(r):
        return wide[r, 0:PROBES, :]

    def probe_row(r):
        return wide[r, PROBES : 2 * PROBES, :]

    half_image(probe_row, 0)
    for i in range(ROWS):
        probe_image[i] = inner[DEPTH + i, :, 0:LANES]
    half_image(warm_row, 7)
    for i in range(ROWS):
        images[i, 0:PROBES, :] = inner[DEPTH + i, :, 0:LANES]

    @pl.loop(DEPTH - 6, DEPTH + ROWS + 6, unroll=2)
    def _(r):
        image = coef[r, 0:1, :] * stencil(inner_row, r) + (1.0 - coef[r, 0:1, :]) * warm_row(r)
        power[0, r] = probe_row(r) - image

    for k in range(3):

        def read(r, k=k):
            return power[k, r]

        half_image(read, 5 - 2 * k)
        for i in range(ROWS):
            images[i, (k + 1) * PROBES : (k + 2) * PROBES, :] = inner[DEPTH + i, :, 0:LANES]

        @pl.loop(DEPTH - (4 - 2 * k), DEPTH + ROWS + (4 - 2 * k), unroll=2)
        def _(r, k=k, read=read):
            power[k + 1, r] = coef[r, 3:4, :] * stencil(inner_row, r) + coef[r, 4:5, :] * read(r)

    for k in range(4):
        for i in range(ROWS):
            basis[i, k * PROBES : (k + 1) * PROBES, :] = power[k, DEPTH + i, :, 0:LANES]

    def add_gram(i, total):
        block = basis[i]
        return total + lax.dot_general(
            block[0 : 3 * PROBES],
            block,
            (((1,), (1,)), ((), ())),
            precision=lax.Precision.HIGHEST,
            preferred_element_type=jnp.float32,
        )

    total = lax.fori_loop(0, ROWS, add_gram, jnp.zeros((3 * PROBES, 4 * PROBES), jnp.float32))
    lane = lax.broadcasted_iota(jnp.int32, (PROBES, LANES), 1)
    row = lax.broadcasted_iota(jnp.int32, (PROBES, LANES), 0)
    packed = jnp.zeros((PROBES, LANES), jnp.float32)
    for b in range(3):
        even = total[b * PROBES : (b + 1) * PROBES]
        odd = pltpu.roll(even, LANES - PROBES, 1)
        column = lane - b * PROBES
        inside = (column >= 0) & (column < PROBES)
        packed = jnp.where(inside, jnp.where(column >= row, even, odd), packed)
        odd_diagonal = jnp.sum(jnp.where(column == row, odd, 0.0), axis=1, keepdims=True)
        packed = jnp.where(lane == 3 * PROBES + b, odd_diagonal, packed)
    sums[...] = packed


def dot(left, right):
    return jnp.dot(left, right, precision=lax.Precision.HIGHEST, preferred_element_type=jnp.float32)


def eliminate(table):
    row = lax.broadcasted_iota(jnp.int32, (PROBES, 1), 0)
    for k in range(PROBES):
        pivot_row = table[k : k + 1, :]
        pivot_row = pivot_row / pivot_row[:, k : k + 1]
        table = jnp.where(row == k, pivot_row, table - table[:, k : k + 1] * pivot_row)
    return table[:, PROBES:]


def finish_kernel(
    sums, low, high, basis, images, probe_image,
    solution_out, residual_out, grad_out,
    coeffs,
):
    packed = sums[...]
    flipped = packed.T
    lane = lax.broadcasted_iota(jnp.int32, (PROBES, PROBES), 1)
    row = lax.broadcasted_iota(jnp.int32, (PROBES, PROBES), 0)
    moments = []
    for b in range(3):
        block = packed[:, b * PROBES : (b + 1) * PROBES]
        mirror = flipped[b * PROBES : (b + 1) * PROBES, :]
        moments.append(jnp.where(lane >= row, block, mirror))
        odd = jnp.where(lane < row, block, mirror)
        moments.append(jnp.where(lane == row, packed[:, 3 * PROBES + b : 3 * PROBES + b + 1], odd))
    power = [moments[k + 1] * (1.0 / GAIN) + moments[k] * SHIFT for k in range(5)]

    first = eliminate(jnp.concatenate([power[0], power[1], power[2], moments[0]], axis=1))
    below = jnp.concatenate([power[1], power[2]], axis=0)
    rest = jnp.concatenate(
        [
            jnp.concatenate([power[2], power[3], moments[1]], axis=1),
            jnp.concatenate([power[3], power[4], moments[2]], axis=1),
        ],
        axis=0,
    )
    rest = rest - dot(below, first)
    second = eliminate(rest[0:PROBES])
    last = rest[PROBES:, PROBES:] - dot(rest[PROBES:, 0:PROBES], second)
    c2 = eliminate(last)
    c1 = second[:, PROBES:] - dot(second[:, 0:PROBES], c2)
    c0 = first[:, 2 * PROBES :] - dot(first[:, 0 : 2 * PROBES], jnp.concatenate([c1, c2], axis=0))

    one = (lane == row).astype(jnp.float32)
    scale = 1.0 / GAIN
    coeffs[0:PROBES, :] = jnp.concatenate([c0.T, c1.T, c2.T, jnp.zeros_like(c0)], axis=1)
    coeffs[PROBES:, :] = jnp.concatenate(
        [(one - SHIFT * c0).T, (-scale * c0 - SHIFT * c1).T, (-scale * c1 - SHIFT * c2).T, (-scale * c2).T], axis=1
    )
    weights = jnp.concatenate([one, c0.T, c1.T, c2.T], axis=1)

    for i in range(ROWS):
        own = low if i < DEPTH else high
        both = dot(coeffs[...], basis[i])
        values = both[0:PROBES] + own[i % DEPTH, 0:PROBES, :]
        solution_out[:, i, :] = values
        residual_out[:, i, :] = both[PROBES:]
        image = dot(weights, images[i])
        terms = values * probe_image[i] + image * own[i % DEPTH, PROBES : 2 * PROBES, :]
        wet = own[i % DEPTH, 64:65, :]
        grad_out[i : i + 1, :] = wet * (jnp.sum(terms, axis=0, keepdims=True) * (1.0 / PROBES))


def f32(*shape):
    return jax.ShapeDtypeStruct(shape, jnp.float32)


def shifted(value, axes, step, wrap):
    size = lax.axis_size(axes)
    if wrap:
        pairs = [(i, (i + step) % size) for i in range(size)]
    else:
        pairs = [(i, i + step) for i in range(size) if 0 <= i + step < size]
    return lax.ppermute(value, axes, pairs)


def spread_sum(value, axes):
    size = lax.axis_size(axes)
    copies = jnp.broadcast_to(value[None], (size,) + value.shape)
    return jnp.sum(lax.all_to_all(copies, axes, 0, 0), axis=0)


def make_local(lat, lon, stages):
    def local(warm_start, probe_signs, ocean_mask, kappa_sq, scale_field):
        low, high, left, right = pl.pallas_call(
            pack_kernel,
            out_shape=(f32(DEPTH, FIELDS, LANES), f32(DEPTH, FIELDS, LANES), f32(FIELDS, LANES), f32(FIELDS, LANES)),
            compiler_params=PARAMS,
            name="pack_edges",
        )(warm_start, probe_signs, ocean_mask, kappa_sq, scale_field)
        from_left = shifted(right, lat, 1, False)
        from_right = shifted(left, lat, -1, False)
        from_prev = shifted(high, lon, 1, True)
        from_next = shifted(low, lon, -1, True)
        first, last = pl.pallas_call(
            corner_kernel,
            out_shape=(f32(FIELDS, LANES), f32(FIELDS, LANES)),
            compiler_params=PARAMS,
            name="pack_corners",
        )(from_left, from_right)
        corner_prev = shifted(last, lon, 1, True)
        corner_next = shifted(first, lon, -1, True)
        tall = ROWS + 2 * DEPTH
        sums, basis, images, probe_image = pl.pallas_call(
            krylov_kernel,
            out_shape=(
                f32(PROBES, LANES),
                f32(ROWS, 4 * PROBES, LANES),
                f32(ROWS, 4 * PROBES, LANES),
                f32(ROWS, PROBES, LANES),
            ),
            scratch_shapes=[
                pltpu.VMEM((tall, FIELDS, 2 * LANES), jnp.float32),
                pltpu.VMEM((4, tall, PROBES, 2 * LANES), jnp.float32),
                pltpu.VMEM((tall, PROBES, 2 * LANES), jnp.float32),
                pltpu.VMEM((tall, 8, 2 * LANES), jnp.float32),
            ],
            compiler_params=PARAMS,
            name="krylov_moments",
        )(low, high, from_left, from_right, from_next, from_prev, corner_next, corner_prev)
        with jax.named_scope("sum_moments"):
            for axes in stages:
                sums = spread_sum(sums, axes)
        return pl.pallas_call(
            finish_kernel,
            out_shape=(
                f32(PROBES, ROWS, LANES),
                f32(PROBES, ROWS, LANES),
                f32(ROWS, LANES),
            ),
            scratch_shapes=[pltpu.VMEM((2 * PROBES, 4 * PROBES), jnp.float32)],
            compiler_params=PARAMS,
            name="solve_and_combine",
        )(sums, low, high, basis, images, probe_image)

    return local


def solution(mesh):
    if mesh.devices.shape == (16, 32):
        grid = Mesh(mesh.devices.reshape(2, 4, 2, 4, 8), ("zh", "x", "c", "zl", "y"))
        lat, lon = (("zh", "x", "c"), ("zl", "y"))
        stages = (("c",), ("x",), ("y",), ("zh", "zl"))
    else:
        grid, lat, lon, stages = (mesh, ("lat",), ("lon",), (("lat",), ("lon",)))
    return jax.shard_map(
        make_local(lat, lon, stages),
        mesh=grid,
        in_specs=(P(None, lon, lat), P(None, lon, lat), P(lon, lat), P(lon, lat), P(lon, lat)),
        out_specs=(P(None, lon, lat), P(None, lon, lat), P(lon, lat)),
        check_vma=False,
    )
```

```python
import jax
import jax.numpy as jnp
from jax import lax
from jax.experimental import pallas as pl
from jax.experimental.pallas import tpu as pltpu
from jax.sharding import Mesh
from jax.sharding import PartitionSpec as P

PROBES = 32
DEPTH = 8
ROWS = 16
LANES = 128
FIELDS = 72
SHIFT = 4.0
GAIN = 0.25
PARAMS = pltpu.CompilerParams(vmem_limit_bytes=48 * 1024 * 1024)


def pack_kernel(warm, signs, mask, kappa, scale, low, high, left, right):
    wet = mask[...].astype(jnp.float32)
    diag = kappa[...] + 4.0
    scaled = scale[...]
    block = lax.broadcasted_iota(jnp.int32, (FIELDS, LANES), 1) // DEPTH
    left_edge = jnp.zeros((FIELDS, LANES), jnp.float32)
    right_edge = jnp.zeros((FIELDS, LANES), jnp.float32)
    for i in range(ROWS):
        out = low if i < DEPTH else high
        j = i % DEPTH
        out[j, 0:PROBES, :] = warm[:, i, :]
        out[j, PROBES : 2 * PROBES, :] = 2.0 * signs[:, i, :].astype(jnp.float32) - 1.0
        out[j, 2 * PROBES :, :] = jnp.concatenate(
            [wet[i : i + 1], diag[i : i + 1], scaled[i : i + 1], jnp.zeros((5, LANES), jnp.float32)], axis=0
        )
        row = out[j]
        turned = pltpu.roll(row, DEPTH * i, 1) if i else row
        left_edge = jnp.where(block == i, turned, left_edge)
        right_edge = jnp.where(block == (i - 1) % ROWS, turned, right_edge)
    left[...] = left_edge
    right[...] = right_edge


def corner_kernel(from_left, from_right, first, last):
    lane = lax.broadcasted_iota(jnp.int32, (FIELDS, LANES), 1)
    before, after = from_left[...], from_right[...]
    first[...] = jnp.where(lane < 64, after, pltpu.roll(before, 72, 1))
    last[...] = jnp.where(lane < 64, pltpu.roll(after, 64, 1), pltpu.roll(before, 8, 1))


def krylov_kernel(
    low, high, from_left, from_right, from_next, from_prev, corner_next, corner_prev,
    sums, basis, images, probe_image,
    wide, power, masked, inner, coef,
):
    lane = lax.broadcasted_iota(jnp.int32, (FIELDS, LANES), 1)
    for r in range(ROWS + 2 * DEPTH):
        i = r - DEPTH
        if i < 0:
            wide[r, :, 0:LANES] = from_prev[r]
            pair = corner_prev[...]
            after, before = (pltpu.roll(pair, (LANES - 8 * r) % LANES, 1), pltpu.roll(pair, (56 - 8 * r) % LANES, 1))
        elif i < ROWS:
            wide[r, :, 0:LANES] = low[i] if i < DEPTH else high[i - DEPTH]
            turn = (LANES - 8 * i) % LANES
            after, before = (pltpu.roll(from_right[...], turn, 1), pltpu.roll(from_left[...], turn, 1))
        else:
            j = i - ROWS
            wide[r, :, 0:LANES] = from_next[j]
            pair = corner_next[...]
            after, before = (pltpu.roll(pair, (LANES - 8 * j) % LANES, 1), pltpu.roll(pair, (56 - 8 * j) % LANES, 1))
        wide[r, :, LANES:] = jnp.where(lane < 64, after, before)
        wet = wide[r, 64:65, :]
        coef[r, 0:1, :] = wet
        coef[r, 1:2, :] = wide[r, 65:66, :]
        coef[r, 2:3, :] = wet * wide[r, 66:67, :]
        coef[r, 3:4, :] = GAIN * wet
        coef[r, 4:5, :] = GAIN * ((1.0 - wet) - SHIFT)

    def stencil(field, r):
        here = field[r]
        around = field[r - 1] + field[r + 1]
        around = around + (pltpu.roll(here, 1, 1) + pltpu.roll(here, 2 * LANES - 1, 1))
        return coef[r, 1:2, :] * here - around

    def half_image(field, reach, keep):
        for r in range(DEPTH - reach, DEPTH + ROWS + reach):
            value = coef[r, 2:3, :] * stencil(field, r)
            inner[r] = value
            if DEPTH <= r < DEPTH + ROWS:
                keep(r - DEPTH, value[:, 0:LANES])

    def keep_images(k):
        def keep(i, value):
            images[i, k * PROBES : (k + 1) * PROBES, :] = value

        return keep

    def keep_probe_image(i, value):
        probe_image[i] = value

    for r in range(DEPTH - 1, DEPTH + ROWS + 1):
        masked[r] = coef[r, 0:1, :] * wide[r, PROBES : 2 * PROBES, :]
    half_image(masked, 0, keep_probe_image)
    for r in range(ROWS + 2 * DEPTH):
        masked[r] = coef[r, 0:1, :] * wide[r, 0:PROBES, :]
    half_image(masked, 7, keep_images(3))

    for k in range(4):
        reach = 6 - 2 * k
        for r in range(DEPTH - reach, DEPTH + ROWS + reach):
            if k == 0:
                image = coef[r, 0:1, :] * stencil(inner, r) + (1.0 - coef[r, 0:1, :]) * wide[r, 0:PROBES, :]
                value = wide[r, PROBES : 2 * PROBES, :] - image
            else:
                value = coef[r, 3:4, :] * stencil(inner, r) + coef[r, 4:5, :] * power[r]
            if k < 3:
                power[r] = value
                masked[r] = coef[r, 0:1, :] * value
            if DEPTH <= r < DEPTH + ROWS:
                basis[r - DEPTH, k * PROBES : (k + 1) * PROBES, :] = value[:, 0:LANES]
        if k < 3:
            half_image(masked, reach - 1, keep_images(k))

    total = jnp.zeros((3 * PROBES, 4 * PROBES), jnp.float32)
    for i in range(ROWS):
        block = basis[i]
        total = total + lax.dot_general(
            block[0 : 3 * PROBES],
            block,
            (((1,), (1,)), ((), ())),
            precision=lax.Precision.HIGH,
            preferred_element_type=jnp.float32,
        )
    lane = lax.broadcasted_iota(jnp.int32, (PROBES, LANES), 1)
    row = lax.broadcasted_iota(jnp.int32, (PROBES, LANES), 0)
    packed = jnp.zeros((PROBES, LANES), jnp.float32)
    for b in range(3):
        even = total[b * PROBES : (b + 1) * PROBES]
        odd = pltpu.roll(even, LANES - PROBES, 1)
        column = lane - b * PROBES
        inside = (column >= 0) & (column < PROBES)
        packed = jnp.where(inside, jnp.where(column >= row, even, odd), packed)
        odd_diagonal = jnp.sum(jnp.where(column == row, odd, 0.0), axis=1, keepdims=True)
        packed = jnp.where(lane == 3 * PROBES + b, odd_diagonal, packed)
    sums[...] = packed


def dot(left, right, precision=lax.Precision.HIGHEST):
    return jnp.dot(left, right, precision=precision, preferred_element_type=jnp.float32)


def eliminate(table, at):
    width = table.shape[1]
    parts = [table[8 * v : 8 * v + 8] for v in range(4)]
    row = lax.broadcasted_iota(jnp.int32, (8, width), 0)

    def spread(value):
        return jnp.broadcast_to(value, (8, width))

    for k in range(0, PROBES, 4):
        home = k // 8
        r = [spread(parts[home][k % 8 + i : k % 8 + i + 1]) for i in range(4)]
        p = {(i, j): spread(r[i][:, at + k + j : at + k + j + 1]) for i in range(4) for j in range(i, 4)}
        columns = [[spread(part[:, at + k + j : at + k + j + 1]) for j in range(4)] for part in parts]
        first = 1.0 / (p[0, 0] * p[1, 1] - p[0, 1] * p[0, 1])
        a00, a01, a11 = (p[1, 1] * first, -p[0, 1] * first, p[0, 0] * first)
        e02, e03 = (a00 * p[0, 2] + a01 * p[1, 2], a00 * p[0, 3] + a01 * p[1, 3])
        e12, e13 = (a01 * p[0, 2] + a11 * p[1, 2], a01 * p[0, 3] + a11 * p[1, 3])
        s00 = p[2, 2] - (p[0, 2] * e02 + p[1, 2] * e12)
        s01 = p[2, 3] - (p[0, 2] * e03 + p[1, 2] * e13)
        s11 = p[3, 3] - (p[0, 3] * e03 + p[1, 3] * e13)
        second = 1.0 / (s00 * s11 - s01 * s01)
        t00, t01, t11 = (s11 * second, -s01 * second, s00 * second)
        y0, y1 = (a00 * r[0] + a01 * r[1], a01 * r[0] + a11 * r[1])
        z2 = r[2] - (p[0, 2] * y0 + p[1, 2] * y1)
        z3 = r[3] - (p[0, 3] * y0 + p[1, 3] * y1)
        x2, x3 = (t00 * z2 + t01 * z3, t01 * z2 + t11 * z3)
        x0, x1 = (y0 - (e02 * x2 + e03 * x3), y1 - (e12 * x2 + e13 * x3))
        solved = (x0, x1, x2, x3)
        parts = [
            part - ((column[0] * x0 + column[1] * x1) + (column[2] * x2 + column[3] * x3))
            for part, column in zip(parts, columns, strict=True)
        ]
        for i in range(4):
            parts[home] = jnp.where(row == k % 8 + i, solved[i], parts[home])
    return jnp.concatenate(parts, axis=0)


def finish_kernel(
    sums, low, high, basis, images, probe_image,
    solution_out, residual_out, grad_out,
    coeffs,
):
    packed = sums[...]
    flipped = packed.T
    lane = lax.broadcasted_iota(jnp.int32, (PROBES, PROBES), 1)
    row = lax.broadcasted_iota(jnp.int32, (PROBES, PROBES), 0)
    moments = []
    for b in range(3):
        block = packed[:, b * PROBES : (b + 1) * PROBES]
        mirror = flipped[b * PROBES : (b + 1) * PROBES, :]
        moments.append(jnp.where(lane >= row, block, mirror))
        odd = jnp.where(lane < row, block, mirror)
        moments.append(jnp.where(lane == row, packed[:, 3 * PROBES + b : 3 * PROBES + b + 1], odd))
    power = [moments[k + 1] * (1.0 / GAIN) + moments[k] * SHIFT for k in range(5)]

    zero = jnp.zeros((PROBES, PROBES), jnp.float32)
    first = eliminate(jnp.concatenate([moments[0], power[2], power[1], power[0]], axis=1), 3 * PROBES)
    first = first[:, 0 : 3 * PROBES]
    rest = jnp.concatenate(
        [
            jnp.concatenate([moments[1], power[3], power[2]], axis=1),
            jnp.concatenate([moments[2], power[4], power[3]], axis=1),
        ],
        axis=0,
    )
    rest = rest - dot(jnp.concatenate([power[1], power[2]], axis=0), first)
    second = eliminate(rest[0:PROBES], 2 * PROBES)[:, 0 : 2 * PROBES]
    nothing = jnp.zeros((2 * PROBES, 2 * PROBES), jnp.float32)
    last = rest[PROBES:, 0 : 2 * PROBES] - dot(rest[PROBES:], jnp.concatenate([nothing, second], axis=0))
    c2 = eliminate(last, PROBES)[:, 0:PROBES]
    c1 = second[:, 0:PROBES] - dot(second, jnp.concatenate([zero, c2], axis=0))
    c0 = first[:, 0:PROBES] - dot(first, jnp.concatenate([zero, c2, c1], axis=0))

    one = (lane == row).astype(jnp.float32)
    scale = 1.0 / GAIN
    columns = jnp.concatenate(
        [
            jnp.concatenate([c0, one - SHIFT * c0], axis=1),
            jnp.concatenate([c1, -scale * c0 - SHIFT * c1], axis=1),
            jnp.concatenate([c2, -scale * c1 - SHIFT * c2], axis=1),
            jnp.concatenate([zero, -scale * c2], axis=1),
        ],
        axis=0,
    )
    coeffs[...] = columns.T
    weights = coeffs[0:PROBES, :] + jnp.concatenate([zero, zero, zero, one], axis=1)

    for i in range(ROWS):
        own = low if i < DEPTH else high
        both = dot(coeffs[...], basis[i], lax.Precision.HIGH)
        values = both[0:PROBES] + own[i % DEPTH, 0:PROBES, :]
        solution_out[:, i, :] = values
        residual_out[:, i, :] = both[PROBES:]
        image = dot(weights, images[i], lax.Precision.HIGH)
        terms = values * probe_image[i] + image * own[i % DEPTH, PROBES : 2 * PROBES, :]
        wet = own[i % DEPTH, 64:65, :]
        grad_out[i : i + 1, :] = wet * (jnp.sum(terms, axis=0, keepdims=True) * (1.0 / PROBES))


def f32(*shape):
    return jax.ShapeDtypeStruct(shape, jnp.float32)


def shifted(value, axes, step, wrap):
    size = lax.axis_size(axes)
    if wrap:
        pairs = [(i, (i + step) % size) for i in range(size)]
    else:
        pairs = [(i, i + step) for i in range(size) if 0 <= i + step < size]
    return lax.ppermute(value, axes, pairs)


def spread_sum(value, axes):
    size = lax.axis_size(axes)
    copies = jnp.broadcast_to(value[None], (size,) + value.shape)
    return jnp.sum(lax.all_to_all(copies, axes, 0, 0), axis=0)


def make_local(lat, lon, stages):
    def local(warm_start, probe_signs, ocean_mask, kappa_sq, scale_field):
        low, high, left, right = pl.pallas_call(
            pack_kernel,
            out_shape=(f32(DEPTH, FIELDS, LANES), f32(DEPTH, FIELDS, LANES), f32(FIELDS, LANES), f32(FIELDS, LANES)),
            compiler_params=PARAMS,
            name="pack_edges",
        )(warm_start, probe_signs, ocean_mask, kappa_sq, scale_field)
        from_left = shifted(right, lat, 1, False)
        from_right = shifted(left, lat, -1, False)
        from_prev = shifted(high, lon, 1, True)
        from_next = shifted(low, lon, -1, True)
        first, last = pl.pallas_call(
            corner_kernel,
            out_shape=(f32(FIELDS, LANES), f32(FIELDS, LANES)),
            compiler_params=PARAMS,
            name="pack_corners",
        )(from_left, from_right)
        corner_prev = shifted(last, lon, 1, True)
        corner_next = shifted(first, lon, -1, True)
        tall = ROWS + 2 * DEPTH
        sums, basis, images, probe_image = pl.pallas_call(
            krylov_kernel,
            out_shape=(
                f32(PROBES, LANES),
                f32(ROWS, 4 * PROBES, LANES),
                f32(ROWS, 4 * PROBES, LANES),
                f32(ROWS, PROBES, LANES),
            ),
            scratch_shapes=[
                pltpu.VMEM((tall, FIELDS, 2 * LANES), jnp.float32),
                pltpu.VMEM((tall, PROBES, 2 * LANES), jnp.float32),
                pltpu.VMEM((tall, PROBES, 2 * LANES), jnp.float32),
                pltpu.VMEM((tall, PROBES, 2 * LANES), jnp.float32),
                pltpu.VMEM((tall, 8, 2 * LANES), jnp.float32),
            ],
            compiler_params=PARAMS,
            name="krylov_moments",
        )(low, high, from_left, from_right, from_next, from_prev, corner_next, corner_prev)
        with jax.named_scope("sum_moments"):
            for axes in stages:
                sums = spread_sum(sums, axes)
        return pl.pallas_call(
            finish_kernel,
            out_shape=(
                f32(PROBES, ROWS, LANES),
                f32(PROBES, ROWS, LANES),
                f32(ROWS, LANES),
            ),
            scratch_shapes=[pltpu.VMEM((2 * PROBES, 4 * PROBES), jnp.float32)],
            compiler_params=PARAMS,
            name="solve_and_combine",
        )(sums, low, high, basis, images, probe_image)

    return local


def solution(mesh):
    if mesh.devices.shape == (16, 32):
        grid = Mesh(mesh.devices.reshape(2, 4, 2, 4, 8), ("zh", "x", "c", "zl", "y"))
        lat, lon = (("zh", "x", "c"), ("zl", "y"))
        stages = (("c",), ("x",), ("y",), ("zh", "zl"))
    else:
        grid, lat, lon, stages = (mesh, ("lat",), ("lon",), (("lat",), ("lon",)))
    return jax.shard_map(
        make_local(lat, lon, stages),
        mesh=grid,
        in_specs=(P(None, lon, lat), P(None, lon, lat), P(lon, lat), P(lon, lat), P(lon, lat)),
        out_specs=(P(None, lon, lat), P(None, lon, lat), P(lon, lat)),
        check_vma=False,
    )
```

```python
import functools

import jax
import jax.numpy as jnp
from jax import lax
from jax.experimental import pallas as pl
from jax.experimental.pallas import tpu as pltpu
from jax.sharding import Mesh
from jax.sharding import PartitionSpec as P

PROBES = 32
DEPTH = 8
ROWS = 16
LANES = 128
FIELDS = 72
SHIFT = 4.0
GAIN = 0.25
PARAMS = pltpu.CompilerParams(vmem_limit_bytes=48 * 1024 * 1024)


def parities(axes):
    return tuple(lax.rem(lax.axis_index(axis), 2) for axis in axes)


def pack_kernel(axes, warm_hbm, signs_hbm, mask_hbm, kappa_hbm, scale_hbm, own, fields, to_even, to_odd, *scratch):
    odd, _ = parities(axes)
    sems = scratch[-1]
    copies = [
        pltpu.make_async_copy(source, target, sems.at[n])
        for n, (source, target) in enumerate(
            zip((warm_hbm, signs_hbm, mask_hbm, kappa_hbm, scale_hbm), scratch[:-1], strict=True)
        )
    ]
    for copy in copies:
        copy.start()
    for copy in copies:
        copy.wait()
    warm, signs, mask, kappa, scale = scratch[:-1]
    wet = mask[...].astype(jnp.float32)
    diag = kappa[...] + 4.0
    scaled = scale[...]
    fields[0] = wet
    fields[1] = diag
    fields[2] = scaled
    block = lax.broadcasted_iota(jnp.int32, (FIELDS, LANES), 1) // DEPTH
    left_edge = jnp.zeros((FIELDS, LANES), jnp.float32)
    right_edge = jnp.zeros((FIELDS, LANES), jnp.float32)
    for i in range(ROWS):
        own[i, 0:PROBES, :] = warm[:, i, :]
        own[i, PROBES : 2 * PROBES, :] = 2.0 * signs[:, i, :].astype(jnp.float32) - 1.0
        own[i, 2 * PROBES :, :] = jnp.concatenate(
            [wet[i : i + 1], diag[i : i + 1], scaled[i : i + 1], jnp.zeros((5, LANES), jnp.float32)], axis=0
        )
        row = own[i]
        turned = pltpu.roll(row, DEPTH * i, 1) if i else row
        left_edge = jnp.where(block == i, turned, left_edge)
        right_edge = jnp.where(block == (i - 1) % ROWS, turned, right_edge)
    to_even[...] = jnp.where(odd == 0, right_edge, left_edge)
    to_odd[...] = jnp.where(odd == 0, left_edge, right_edge)


def sides(odd, even_side, odd_side):
    return jnp.where(odd == 0, odd_side, even_side), jnp.where(odd == 0, even_side, odd_side)


SEND_PROBES = DEPTH * PROBES
SEND_FIELDS = SEND_PROBES + (DEPTH - 2) * PROBES
SEND_CORNER = SEND_FIELDS + 3 * DEPTH
SEND_ROWS = SEND_CORNER + FIELDS


def send_kernel(axes, own, fields, from_even, from_odd, to_even, to_odd):
    odd_lat, odd_lon = parities(axes)
    lane = lax.broadcasted_iota(jnp.int32, (FIELDS, LANES), 1)
    before, after = sides(odd_lat, from_even[...], from_odd[...])
    first = jnp.where(lane < 64, after, pltpu.roll(before, 72, 1))
    last = jnp.where(lane < 64, pltpu.roll(after, 64, 1), pltpu.roll(before, 8, 1))
    for target, is_last in ((to_even, odd_lon == 0), (to_odd, odd_lon != 0)):
        start = jnp.where(is_last, DEPTH, 0)
        near = jnp.where(is_last, DEPTH + 2, 0)
        for j in range(DEPTH):
            target[j * PROBES : (j + 1) * PROBES, :] = own[start + j, 0:PROBES, :]
        for j in range(DEPTH - 2):
            target[SEND_PROBES + j * PROBES : SEND_PROBES + (j + 1) * PROBES, :] = own[near + j, PROBES : 2 * PROBES, :]
        for f in range(3):
            target[SEND_FIELDS + f * DEPTH : SEND_FIELDS + (f + 1) * DEPTH, :] = jnp.where(
                is_last, fields[f, DEPTH:, :], fields[f, 0:DEPTH, :]
            )
        target[SEND_CORNER:, :] = jnp.where(is_last, last, first)


def krylov_kernel(
    axes,
    own, from_even_lat, from_odd_lat, from_even_lon, from_odd_lon,
    sums, basis, images, probe_image,
    wide, power, masked, inner, coef,
):
    odd_lat, odd_lon = parities(axes)
    lane = lax.broadcasted_iota(jnp.int32, (FIELDS, LANES), 1)
    before, after = sides(odd_lat, from_even_lat[...], from_odd_lat[...])
    for i in range(ROWS):
        turn = (LANES - 8 * i) % LANES
        wide[DEPTH + i, :, 0:LANES] = own[i]
        wide[DEPTH + i, :, LANES:] = jnp.where(lane < 64, pltpu.roll(after, turn, 1), pltpu.roll(before, turn, 1))
    for side, is_next in ((from_even_lon, odd_lon == 0), (from_odd_lon, odd_lon != 0)):
        start = jnp.where(is_next, DEPTH + ROWS, 0)
        near = jnp.where(is_next, DEPTH + ROWS, 2)
        pair = side[SEND_CORNER:, :]
        for j in range(DEPTH):
            wide[start + j, 0:PROBES, 0:LANES] = side[j * PROBES : (j + 1) * PROBES, :]
            for f in range(3):
                at = SEND_FIELDS + f * DEPTH + j
                wide[start + j, 2 * PROBES + f : 2 * PROBES + f + 1, 0:LANES] = side[at : at + 1, :]
            wide[start + j, :, LANES:] = jnp.where(
                lane < 64, pltpu.roll(pair, (LANES - 8 * j) % LANES, 1), pltpu.roll(pair, (56 - 8 * j) % LANES, 1)
            )
        for j in range(DEPTH - 2):
            at = SEND_PROBES + j * PROBES
            wide[near + j, PROBES : 2 * PROBES, 0:LANES] = side[at : at + PROBES, :]
    for r in range(ROWS + 2 * DEPTH):
        wet = wide[r, 64:65, :]
        coef[r, 0:1, :] = wet
        coef[r, 1:2, :] = wide[r, 65:66, :]
        coef[r, 2:3, :] = wet * wide[r, 66:67, :]
        coef[r, 3:4, :] = GAIN * wet
        coef[r, 4:5, :] = GAIN * ((1.0 - wet) - SHIFT)

    def stencil(field, r):
        here = field[r]
        around = field[r - 1] + field[r + 1]
        around = around + (pltpu.roll(here, 1, 1) + pltpu.roll(here, 2 * LANES - 1, 1))
        return coef[r, 1:2, :] * here - around

    def half_image(field, reach, keep):
        for r in range(DEPTH - reach, DEPTH + ROWS + reach):
            value = coef[r, 2:3, :] * stencil(field, r)
            inner[r] = value
            if DEPTH <= r < DEPTH + ROWS:
                keep(r - DEPTH, value[:, 0:LANES])

    def keep_images(k):
        def keep(i, value):
            images[i, k * PROBES : (k + 1) * PROBES, :] = value

        return keep

    def keep_probe_image(i, value):
        probe_image[i] = value

    for r in range(DEPTH - 1, DEPTH + ROWS + 1):
        masked[r] = coef[r, 0:1, :] * wide[r, PROBES : 2 * PROBES, :]
    half_image(masked, 0, keep_probe_image)
    for r in range(ROWS + 2 * DEPTH):
        masked[r] = coef[r, 0:1, :] * wide[r, 0:PROBES, :]
    half_image(masked, 7, keep_images(3))

    for k in range(4):
        reach = 6 - 2 * k
        for r in range(DEPTH - reach, DEPTH + ROWS + reach):
            if k == 0:
                image = coef[r, 0:1, :] * stencil(inner, r) + (1.0 - coef[r, 0:1, :]) * wide[r, 0:PROBES, :]
                value = wide[r, PROBES : 2 * PROBES, :] - image
            else:
                value = coef[r, 3:4, :] * stencil(inner, r) + coef[r, 4:5, :] * power[r]
            if k < 3:
                power[r] = value
                masked[r] = coef[r, 0:1, :] * value
            if DEPTH <= r < DEPTH + ROWS:
                basis[r - DEPTH, k * PROBES : (k + 1) * PROBES, :] = value[:, 0:LANES]
        if k < 3:
            half_image(masked, reach - 1, keep_images(k))

    total = jnp.zeros((3 * PROBES, 4 * PROBES), jnp.float32)
    for i in range(ROWS):
        block = basis[i]
        total = total + lax.dot_general(
            block[0 : 3 * PROBES],
            block,
            (((1,), (1,)), ((), ())),
            precision=lax.Precision.HIGH,
            preferred_element_type=jnp.float32,
        )
    lane = lax.broadcasted_iota(jnp.int32, (PROBES, LANES), 1)
    row = lax.broadcasted_iota(jnp.int32, (PROBES, LANES), 0)
    packed = jnp.zeros((PROBES, LANES), jnp.float32)
    for b in range(3):
        even = total[b * PROBES : (b + 1) * PROBES]
        odd = pltpu.roll(even, LANES - PROBES, 1)
        column = lane - b * PROBES
        inside = (column >= 0) & (column < PROBES)
        packed = jnp.where(inside, jnp.where(column >= row, even, odd), packed)
        odd_diagonal = jnp.sum(jnp.where(column == row, odd, 0.0), axis=1, keepdims=True)
        packed = jnp.where(lane == 3 * PROBES + b, odd_diagonal, packed)
    sums[...] = packed


def dot(left, right, precision=lax.Precision.HIGHEST):
    return jnp.dot(left, right, precision=precision, preferred_element_type=jnp.float32)


def eliminate(table, at):
    width = table.shape[1]
    parts = [table[8 * v : 8 * v + 8] for v in range(4)]
    row = lax.broadcasted_iota(jnp.int32, (8, width), 0)

    def spread(value):
        return jnp.broadcast_to(value, (8, width))

    for k in range(0, PROBES, 4):
        home = k // 8
        r = [spread(parts[home][k % 8 + i : k % 8 + i + 1]) for i in range(4)]
        p = {(i, j): spread(r[i][:, at + k + j : at + k + j + 1]) for i in range(4) for j in range(i, 4)}
        columns = [[spread(part[:, at + k + j : at + k + j + 1]) for j in range(4)] for part in parts]
        first = 1.0 / (p[0, 0] * p[1, 1] - p[0, 1] * p[0, 1])
        a00, a01, a11 = (p[1, 1] * first, -p[0, 1] * first, p[0, 0] * first)
        e02, e03 = (a00 * p[0, 2] + a01 * p[1, 2], a00 * p[0, 3] + a01 * p[1, 3])
        e12, e13 = (a01 * p[0, 2] + a11 * p[1, 2], a01 * p[0, 3] + a11 * p[1, 3])
        s00 = p[2, 2] - (p[0, 2] * e02 + p[1, 2] * e12)
        s01 = p[2, 3] - (p[0, 2] * e03 + p[1, 2] * e13)
        s11 = p[3, 3] - (p[0, 3] * e03 + p[1, 3] * e13)
        second = 1.0 / (s00 * s11 - s01 * s01)
        t00, t01, t11 = (s11 * second, -s01 * second, s00 * second)
        y0, y1 = (a00 * r[0] + a01 * r[1], a01 * r[0] + a11 * r[1])
        z2 = r[2] - (p[0, 2] * y0 + p[1, 2] * y1)
        z3 = r[3] - (p[0, 3] * y0 + p[1, 3] * y1)
        x2, x3 = (t00 * z2 + t01 * z3, t01 * z2 + t11 * z3)
        x0, x1 = (y0 - (e02 * x2 + e03 * x3), y1 - (e12 * x2 + e13 * x3))
        solved = (x0, x1, x2, x3)
        parts = [
            part - ((column[0] * x0 + column[1] * x1) + (column[2] * x2 + column[3] * x3))
            for part, column in zip(parts, columns, strict=True)
        ]
        for i in range(4):
            parts[home] = jnp.where(row == k % 8 + i, solved[i], parts[home])
    return jnp.concatenate(parts, axis=0)


def finish_kernel(
    sums, own, basis, images, probe_image,
    solution_out, residual_out, grad_out,
    coeffs,
):
    packed = sums[...]
    flipped = packed.T
    lane = lax.broadcasted_iota(jnp.int32, (PROBES, PROBES), 1)
    row = lax.broadcasted_iota(jnp.int32, (PROBES, PROBES), 0)
    moments = []
    for b in range(3):
        block = packed[:, b * PROBES : (b + 1) * PROBES]
        mirror = flipped[b * PROBES : (b + 1) * PROBES, :]
        moments.append(jnp.where(lane >= row, block, mirror))
        odd = jnp.where(lane < row, block, mirror)
        moments.append(jnp.where(lane == row, packed[:, 3 * PROBES + b : 3 * PROBES + b + 1], odd))
    power = [moments[k + 1] * (1.0 / GAIN) + moments[k] * SHIFT for k in range(5)]

    zero = jnp.zeros((PROBES, PROBES), jnp.float32)
    first = eliminate(jnp.concatenate([moments[0], power[2], power[1], power[0]], axis=1), 3 * PROBES)
    first = first[:, 0 : 3 * PROBES]
    rest = jnp.concatenate(
        [
            jnp.concatenate([moments[1], power[3], power[2]], axis=1),
            jnp.concatenate([moments[2], power[4], power[3]], axis=1),
        ],
        axis=0,
    )
    rest = rest - dot(jnp.concatenate([power[1], power[2]], axis=0), first)
    second = eliminate(rest[0:PROBES], 2 * PROBES)[:, 0 : 2 * PROBES]
    nothing = jnp.zeros((2 * PROBES, 2 * PROBES), jnp.float32)
    last = rest[PROBES:, 0 : 2 * PROBES] - dot(rest[PROBES:], jnp.concatenate([nothing, second], axis=0))
    c2 = eliminate(last, PROBES)[:, 0:PROBES]
    c1 = second[:, 0:PROBES] - dot(second, jnp.concatenate([zero, c2], axis=0))
    c0 = first[:, 0:PROBES] - dot(first, jnp.concatenate([zero, c2, c1], axis=0))

    one = (lane == row).astype(jnp.float32)
    scale = 1.0 / GAIN
    columns = jnp.concatenate(
        [
            jnp.concatenate([c0, one - SHIFT * c0], axis=1),
            jnp.concatenate([c1, -scale * c0 - SHIFT * c1], axis=1),
            jnp.concatenate([c2, -scale * c1 - SHIFT * c2], axis=1),
            jnp.concatenate([zero, -scale * c2], axis=1),
        ],
        axis=0,
    )
    coeffs[...] = columns.T
    weights = coeffs[0:PROBES, :] + jnp.concatenate([zero, zero, zero, one], axis=1)

    for i in range(ROWS):
        both = dot(coeffs[...], basis[i], lax.Precision.HIGH)
        values = both[0:PROBES] + own[i, 0:PROBES, :]
        solution_out[:, i, :] = values
        residual_out[:, i, :] = both[PROBES:]
        image = dot(weights, images[i], lax.Precision.HIGH)
        terms = values * probe_image[i] + image * own[i, PROBES : 2 * PROBES, :]
        wet = own[i, 64:65, :]
        grad_out[i : i + 1, :] = wet * (jnp.sum(terms, axis=0, keepdims=True) * (1.0 / PROBES))


def f32(*shape):
    return jax.ShapeDtypeStruct(shape, jnp.float32)


def exchanged(value, axes, odd, wrap):
    size = lax.axis_size(axes)
    pairs = []
    for i in range(size):
        other = ((i + odd) ^ 1) - odd
        if wrap or 0 <= other < size:
            pairs.append((i, other % size))
    return lax.ppermute(value, axes, pairs)


def spread_sum(value, axes):
    size = lax.axis_size(axes)
    copies = jnp.broadcast_to(value[None], (size,) + value.shape)
    return jnp.sum(lax.all_to_all(copies, axes, 0, 0), axis=0)


def make_local(lat, lon, stages):
    axes = (lat[-1], lon[-1])

    def local(warm_start, probe_signs, ocean_mask, kappa_sq, scale_field):
        args = (warm_start, probe_signs, ocean_mask, kappa_sq, scale_field)
        own, fields, to_even, to_odd = pl.pallas_call(
            functools.partial(pack_kernel, axes),
            out_shape=(
                f32(ROWS, FIELDS, LANES),
                f32(3, ROWS, LANES),
                f32(FIELDS, LANES),
                f32(FIELDS, LANES),
            ),
            in_specs=[pl.BlockSpec(memory_space=pl.ANY)] * 5,
            scratch_shapes=[pltpu.VMEM(x.shape, x.dtype) for x in args] + [pltpu.SemaphoreType.DMA((5,))],
            compiler_params=PARAMS,
            name="pack_edges",
        )(*args)
        odd_lat = exchanged(to_odd, lat, 1, False)
        even_lat = exchanged(to_even, lat, 0, False)
        to_even, to_odd = pl.pallas_call(
            functools.partial(send_kernel, axes),
            out_shape=(f32(SEND_ROWS, LANES), f32(SEND_ROWS, LANES)),
            compiler_params=PARAMS,
            name="pack_rows",
        )(own, fields, even_lat, odd_lat)
        odd_lon = exchanged(to_odd, lon, 1, True)
        even_lon = exchanged(to_even, lon, 0, True)
        tall = ROWS + 2 * DEPTH
        sums, basis, images, probe_image = pl.pallas_call(
            functools.partial(krylov_kernel, axes),
            out_shape=(
                f32(PROBES, LANES),
                f32(ROWS, 4 * PROBES, LANES),
                f32(ROWS, 4 * PROBES, LANES),
                f32(ROWS, PROBES, LANES),
            ),
            scratch_shapes=[
                pltpu.VMEM((tall, FIELDS, 2 * LANES), jnp.float32),
                pltpu.VMEM((tall, PROBES, 2 * LANES), jnp.float32),
                pltpu.VMEM((tall, PROBES, 2 * LANES), jnp.float32),
                pltpu.VMEM((tall, PROBES, 2 * LANES), jnp.float32),
                pltpu.VMEM((tall, 8, 2 * LANES), jnp.float32),
            ],
            compiler_params=PARAMS,
            name="krylov_moments",
        )(own, even_lat, odd_lat, even_lon, odd_lon)
        with jax.named_scope("sum_moments"):
            for group in stages:
                sums = spread_sum(sums, group)
        return pl.pallas_call(
            finish_kernel,
            out_shape=(
                f32(PROBES, ROWS, LANES),
                f32(PROBES, ROWS, LANES),
                f32(ROWS, LANES),
            ),
            scratch_shapes=[pltpu.VMEM((2 * PROBES, 4 * PROBES), jnp.float32)],
            compiler_params=PARAMS,
            name="solve_and_combine",
        )(sums, own, basis, images, probe_image)

    return local


def solution(mesh):
    if mesh.devices.shape == (16, 32):
        grid = Mesh(mesh.devices.reshape(2, 4, 2, 4, 8), ("zh", "x", "c", "zl", "y"))
        lat, lon = (("zh", "x", "c"), ("zl", "y"))
        stages = (("x", "c"), ("y",), ("zh", "zl"))
    else:
        grid, lat, lon, stages = (mesh, ("lat",), ("lon",), (("lat",), ("lon",)))
    return jax.shard_map(
        make_local(lat, lon, stages),
        mesh=grid,
        in_specs=(P(None, lon, lat), P(None, lon, lat), P(lon, lat), P(lon, lat), P(lon, lat)),
        out_specs=(P(None, lon, lat), P(None, lon, lat), P(lon, lat)),
        check_vma=False,
    )
```

```python
import functools

import jax
import jax.numpy as jnp
from jax import lax
from jax.experimental import pallas as pl
from jax.experimental.pallas import tpu as pltpu
from jax.sharding import Mesh
from jax.sharding import PartitionSpec as P

PROBES = 32
DEPTH = 8
ROWS = 16
LANES = 128
FIELDS = 72
SHIFT = 4.0
GAIN = 0.25
PARAMS = pltpu.CompilerParams(vmem_limit_bytes=32 * 1024 * 1024)
ALL_PARAMS = pltpu.CompilerParams(vmem_limit_bytes=60 * 1024 * 1024)


def parities(axes):
    return tuple(lax.rem(lax.axis_index(axis), 2) for axis in axes)


def pack_kernel(axes, warm_hbm, signs_hbm, mask_hbm, kappa_hbm, scale_hbm, own, fields, to_odd, to_even, *scratch):
    odd, _ = parities(axes)
    sems = scratch[-1]
    copies = [
        pltpu.make_async_copy(source, target, sems.at[n])
        for n, (source, target) in enumerate(
            zip((warm_hbm, signs_hbm, mask_hbm, kappa_hbm, scale_hbm), scratch[:-1], strict=True)
        )
    ]
    for copy in copies:
        copy.start()
    for copy in copies:
        copy.wait()
    warm, signs, mask, kappa, scale = scratch[:-1]
    wet = mask[...].astype(jnp.float32)
    diag = kappa[...] + 4.0
    scaled = scale[...]
    fields[0] = wet
    fields[1] = diag
    fields[2] = scaled
    block = lax.broadcasted_iota(jnp.int32, (FIELDS, LANES), 1) // DEPTH
    left_edge = jnp.zeros((FIELDS, LANES), jnp.float32)
    right_edge = jnp.zeros((FIELDS, LANES), jnp.float32)
    for i in range(ROWS):
        own[i, 0:PROBES, :] = warm[:, i, :]
        own[i, PROBES : 2 * PROBES, :] = 2.0 * signs[:, i, :].astype(jnp.float32) - 1.0
        own[i, 2 * PROBES :, :] = jnp.concatenate(
            [wet[i : i + 1], diag[i : i + 1], scaled[i : i + 1], jnp.zeros((5, LANES), jnp.float32)], axis=0
        )
        row = own[i]
        turned = pltpu.roll(row, DEPTH * i, 1) if i else row
        left_edge = jnp.where(block == i, turned, left_edge)
        right_edge = jnp.where(block == (i - 1) % ROWS, turned, right_edge)
    to_even[...] = jnp.where(odd == 0, right_edge, left_edge)
    to_odd[...] = jnp.where(odd == 0, left_edge, right_edge)


def sides(odd, even_side, odd_side):
    return jnp.where(odd == 0, odd_side, even_side), jnp.where(odd == 0, even_side, odd_side)


SEND_PROBES = DEPTH * PROBES
SEND_FIELDS = SEND_PROBES + (DEPTH - 2) * PROBES
SEND_CORNER = SEND_FIELDS + 3 * DEPTH
SEND_ROWS = SEND_CORNER + FIELDS


def send_kernel(axes, own, fields, from_odd, from_even, to_odd, to_even):
    odd_lat, odd_lon = parities(axes)
    lane = lax.broadcasted_iota(jnp.int32, (FIELDS, LANES), 1)
    before, after = sides(odd_lat, from_even[...], from_odd[...])
    first = jnp.where(lane < 64, after, pltpu.roll(before, 72, 1))
    last = jnp.where(lane < 64, pltpu.roll(after, 64, 1), pltpu.roll(before, 8, 1))
    for target, is_last in ((to_even, odd_lon == 0), (to_odd, odd_lon != 0)):
        start = jnp.where(is_last, DEPTH, 0)
        near = jnp.where(is_last, DEPTH + 2, 0)
        for j in range(DEPTH):
            target[j * PROBES : (j + 1) * PROBES, :] = own[start + j, 0:PROBES, :]
        for j in range(DEPTH - 2):
            target[SEND_PROBES + j * PROBES : SEND_PROBES + (j + 1) * PROBES, :] = own[near + j, PROBES : 2 * PROBES, :]
        for f in range(3):
            target[SEND_FIELDS + f * DEPTH : SEND_FIELDS + (f + 1) * DEPTH, :] = jnp.where(
                is_last, fields[f, DEPTH:, :], fields[f, 0:DEPTH, :]
            )
        target[SEND_CORNER:, :] = jnp.where(is_last, last, first)


TALL = ROWS + 2 * DEPTH
INSIDE = dict(mp=(8, 24), up=(9, 23), mw=(8, 24), i0=(9, 23), p0=(10, 22), m0=(10, 22), i1=(11, 21), p1=(12, 20), m1=(12, 20), i2=(13, 19), p2=(14, 18), m2=(14, 18), i3=(15, 17))
NEEDED = dict(mp=(7, 25), up=(8, 24), mw=(0, 32), i0=(1, 31), p0=(2, 30), m0=(2, 30), i1=(3, 29), p1=(4, 28), m1=(4, 28), i2=(5, 27), p2=(6, 26), m2=(6, 26), i3=(7, 25), p3=(8, 24))
HELD = tuple(INSIDE)


def fill_coef(coef, at, wet, diag, scaled):
    coef[at, 0:1, :] = wet
    coef[at, 1:2, :] = diag
    coef[at, 2:3, :] = wet * scaled
    coef[at, 3:4, :] = GAIN * wet
    coef[at, 4:5, :] = GAIN * ((1.0 - wet) - SHIFT)


def march(rows, coef, warm, probe, get, put):
    def stencil(name, r):
        here = get(name, r)
        around = get(name, r - 1) + get(name, r + 1)
        around = around + (pltpu.roll(here, 1, 1) + pltpu.roll(here, 2 * LANES - 1, 1))
        return coef(r, 1) * here - around

    for r in rows("mp"):
        put("mp", r, coef(r, 0) * probe(r))
    for r in rows("mw"):
        put("mw", r, coef(r, 0) * warm(r))
    for r in rows("i0"):
        put("i0", r, coef(r, 2) * stencil("mw", r))
    for r in rows("up"):
        put("up", r, coef(r, 2) * stencil("mp", r))
    for k in range(4):
        power = f"p{k}"
        for r in rows(power):
            if k == 0:
                value = probe(r) - (coef(r, 0) * stencil("i0", r) + (1.0 - coef(r, 0)) * warm(r))
            else:
                value = coef(r, 3) * stencil(f"i{k}", r) + coef(r, 4) * get(f"p{k - 1}", r)
            put(power, r, value)
            if k < 3:
                put(f"m{k}", r, coef(r, 0) * value)
        for r in rows(f"i{k + 1}"):
            put(f"i{k + 1}", r, coef(r, 2) * stencil(f"m{k}", r))


def inside_kernel(axes, own, from_odd, from_even, wide, coefs, *held):
    odd_lat, _ = parities(axes)
    held = dict(zip(HELD, held, strict=True))
    lane = lax.broadcasted_iota(jnp.int32, (FIELDS, LANES), 1)
    before, after = sides(odd_lat, from_even[...], from_odd[...])
    for i in range(ROWS):
        turn = (LANES - 8 * i) % LANES
        wide[i, :, 0:LANES] = own[i]
        wide[i, :, LANES:] = jnp.where(lane < 64, pltpu.roll(after, turn, 1), pltpu.roll(before, turn, 1))
        fill_coef(coefs, i, wide[i, 64:65, :], wide[i, 65:66, :], wide[i, 66:67, :])

    def put(name, r, value):
        held[name][r - DEPTH] = value

    march(
        lambda name: range(*INSIDE.get(name, (0, 0))),
        lambda r, n: coefs[r - DEPTH, n : n + 1, :],
        lambda r: wide[r - DEPTH, 0:PROBES, :],
        lambda r: wide[r - DEPTH, PROBES : 2 * PROBES, :],
        lambda name, r: held[name][r - DEPTH],
        put,
    )


def krylov_kernel(axes, own_wide, own_coefs, *refs):
    held = dict(zip(HELD, refs, strict=False))
    from_odd_lon, from_even_lon, sums, basis, images, probe_image, wide, coefs = refs[len(HELD) : len(HELD) + 8]
    fresh = dict(zip(NEEDED, refs[len(HELD) + 8 :], strict=True))
    _, odd_lon = parities(axes)
    lane = lax.broadcasted_iota(jnp.int32, (FIELDS, LANES), 1)
    for side, is_next in ((from_even_lon, odd_lon == 0), (from_odd_lon, odd_lon != 0)):
        start = jnp.where(is_next, DEPTH + ROWS, 0)
        near = jnp.where(is_next, DEPTH + ROWS, 2)
        pair = side[SEND_CORNER:, :]
        for j in range(DEPTH):
            wide[start + j, 0:PROBES, 0:LANES] = side[j * PROBES : (j + 1) * PROBES, :]
            for f in range(3):
                at = SEND_FIELDS + f * DEPTH + j
                wide[start + j, 2 * PROBES + f : 2 * PROBES + f + 1, 0:LANES] = side[at : at + 1, :]
            wide[start + j, :, LANES:] = jnp.where(
                lane < 64, pltpu.roll(pair, (LANES - 8 * j) % LANES, 1), pltpu.roll(pair, (56 - 8 * j) % LANES, 1)
            )
        for j in range(DEPTH - 2):
            at = SEND_PROBES + j * PROBES
            wide[near + j, PROBES : 2 * PROBES, 0:LANES] = side[at : at + PROBES, :]

    def own(r):
        return DEPTH <= r < DEPTH + ROWS

    for r in range(TALL):
        if not own(r):
            fill_coef(coefs, r, wide[r, 64:65, :], wide[r, 65:66, :], wide[r, 66:67, :])

    def rows(name):
        done = range(*INSIDE.get(name, (0, 0)))
        return [r for r in range(*NEEDED.get(name, (0, 0))) if r not in done]

    def get(name, r):
        return held[name][r - DEPTH] if r in range(*INSIDE.get(name, (0, 0))) else fresh[name][r]

    def put(name, r, value):
        fresh[name][r] = value

    def coef(r, n):
        return own_coefs[r - DEPTH, n : n + 1, :] if own(r) else coefs[r, n : n + 1, :]

    def argument(r, at):
        if own(r):
            return own_wide[r - DEPTH, at : at + PROBES, :]
        return wide[r, at : at + PROBES, :]

    march(rows, coef, lambda r: argument(r, 0), lambda r: argument(r, PROBES), get, put)

    total = jnp.zeros((3 * PROBES, 4 * PROBES), jnp.float32)
    for i in range(ROWS):
        r = DEPTH + i
        for k in range(4):
            at = slice(k * PROBES, (k + 1) * PROBES)
            basis[i, at, :] = get(f"p{k}", r)[:, 0:LANES]
            images[i, at, :] = get(f"i{(k + 1) % 4}", r)[:, 0:LANES]
        probe_image[i] = get("up", r)[:, 0:LANES]
        block = basis[i]
        total = total + lax.dot_general(
            block[0 : 3 * PROBES],
            block,
            (((1,), (1,)), ((), ())),
            precision=lax.Precision.HIGH,
            preferred_element_type=jnp.float32,
        )
    lane = lax.broadcasted_iota(jnp.int32, (PROBES, LANES), 1)
    row = lax.broadcasted_iota(jnp.int32, (PROBES, LANES), 0)
    packed = jnp.zeros((PROBES, LANES), jnp.float32)
    for b in range(3):
        even = total[b * PROBES : (b + 1) * PROBES]
        odd = pltpu.roll(even, LANES - PROBES, 1)
        column = lane - b * PROBES
        inside = (column >= 0) & (column < PROBES)
        packed = jnp.where(inside, jnp.where(column >= row, even, odd), packed)
        odd_diagonal = jnp.sum(jnp.where(column == row, odd, 0.0), axis=1, keepdims=True)
        packed = jnp.where(lane == 3 * PROBES + b, odd_diagonal, packed)
    sums[...] = packed


def dot(left, right):
    return jnp.dot(left, right, precision=lax.Precision.HIGH, preferred_element_type=jnp.float32)


def invert_pair(p):
    scale = 1.0 / (p[0][0] * p[1][1] - p[0][1] * p[0][1])
    return p[1][1] * scale, -p[0][1] * scale, p[0][0] * scale


def prepare(p):
    n = len(p)
    if n == 2:
        a, b, c = invert_pair(p)
        return lambda r: [a * r[0] + b * r[1], b * r[0] + c * r[1]]
    h = n // 2
    top = prepare([row[:h] for row in p[:h]])
    side = [row[h:] for row in p[:h]]
    solved = list(zip(*[top([side[i][j] for i in range(h)]) for j in range(h)], strict=True))

    def product(rows, weights):
        terms = [row * weight for row, weight in zip(rows, weights, strict=True)]
        while len(terms) > 1:
            terms = [sum(terms[i : i + 2][1:], terms[i]) for i in range(0, len(terms), 2)]
        return terms[0]

    rest = [[None] * h for _ in range(h)]
    for i in range(h):
        for j in range(i, h):
            rest[i][j] = p[h + i][h + j] - product([side[t][i] for t in range(h)], [solved[t][j] for t in range(h)])
            rest[j][i] = rest[i][j]
    bottom = prepare(rest)

    def solve(r):
        upper = top(r[:h])
        lower = bottom([r[h + i] - product([side[t][i] for t in range(h)], upper) for i in range(h)])
        return [upper[t] - product(solved[t], lower) for t in range(h)] + lower

    return solve


def eliminate(parts):
    row = lax.broadcasted_iota(jnp.int32, (8, LANES), 0)

    def spread(value):
        return jnp.broadcast_to(value, (8, LANES))

    for home in range(len(parts)):
        at = 8 * home
        columns = [[spread(part[:, at + j : at + j + 1]) for j in range(8)] for part in parts]
        pivot = [[spread(columns[home][j][i : i + 1]) for j in range(8)] for i in range(8)]
        solved = prepare(pivot)([spread(parts[home][i : i + 1]) for i in range(8)])
        for v, column in enumerate(columns):
            if v == home:
                part = solved[0]
                for i in range(1, 8):
                    part = jnp.where(row == i, solved[i], part)
                parts[v] = part
            else:
                terms = [c * x for c, x in zip(column, solved, strict=True)]
                parts[v] = parts[v] - (
                    ((terms[0] + terms[1]) + (terms[2] + terms[3])) + ((terms[4] + terms[5]) + (terms[6] + terms[7]))
                )
    return parts


def finish_kernel(
    sums, own, basis, images, probe_image,
    solution_out, residual_out, grad_out,
    coeffs,
):
    packed = sums[...]
    flipped = packed.T
    lane = lax.broadcasted_iota(jnp.int32, (PROBES, PROBES), 1)
    row = lax.broadcasted_iota(jnp.int32, (PROBES, PROBES), 0)
    moments = []
    for b in range(3):
        block = packed[:, b * PROBES : (b + 1) * PROBES]
        mirror = flipped[b * PROBES : (b + 1) * PROBES, :]
        moments.append(jnp.where(lane >= row, block, mirror))
        odd = jnp.where(lane < row, block, mirror)
        moments.append(jnp.where(lane == row, packed[:, 3 * PROBES + b : 3 * PROBES + b + 1], odd))
    power = [moments[k + 1] * (1.0 / GAIN) + moments[k] * SHIFT for k in range(5)]

    table = jnp.concatenate(
        [jnp.concatenate([power[b], power[b + 1], power[b + 2], moments[b]], axis=1) for b in range(3)], axis=0
    )
    parts = eliminate([table[8 * v : 8 * v + 8] for v in range(12)])
    solved = jnp.concatenate(parts, axis=0)

    nothing = jnp.zeros((PROBES, LANES), jnp.float32)
    wide_lane = lax.broadcasted_iota(jnp.int32, (4 * PROBES, LANES), 1)
    wide_row = lax.broadcasted_iota(jnp.int32, (4 * PROBES, LANES), 0)
    one = (wide_lane == wide_row + 3 * PROBES).astype(jnp.float32)
    kept = jnp.concatenate([solved, nothing], axis=0)
    left = one - SHIFT * kept - (1.0 / GAIN) * jnp.concatenate([nothing, solved], axis=0)
    columns = jnp.where(wide_lane < PROBES, pltpu.roll(kept, PROBES, 1), pltpu.roll(left, 2 * PROBES, 1))
    coeffs[...] = columns.T[0 : 2 * PROBES]
    weights = coeffs[0:PROBES, :] + one[0:PROBES]

    for i in range(ROWS):
        both = dot(coeffs[...], basis[i])
        values = both[0:PROBES] + own[i, 0:PROBES, :]
        solution_out[:, i, :] = values
        residual_out[:, i, :] = both[PROBES:]
        image = dot(weights, images[i])
        terms = values * probe_image[i] + image * own[i, PROBES : 2 * PROBES, :]
        wet = own[i, 64:65, :]
        grad_out[i : i + 1, :] = wet * (jnp.sum(terms, axis=0, keepdims=True) * (1.0 / PROBES))


def f32(*shape):
    return jax.ShapeDtypeStruct(shape, jnp.float32)


def exchanged(value, axes, odd, wrap):
    size = lax.axis_size(axes)
    pairs = []
    for i in range(size):
        other = ((i + odd) ^ 1) - odd
        if wrap or 0 <= other < size:
            pairs.append((i, other % size))
    return lax.ppermute(value, axes, pairs)


def spread_sum(value, axes):
    size = lax.axis_size(axes)
    copies = jnp.broadcast_to(value[None], (size,) + value.shape)
    return jnp.sum(lax.all_to_all(copies, axes, 0, 0), axis=0)


def make_local(lat, lon, stages):
    axes = (lat[-1], lon[-1])

    def local(warm_start, probe_signs, ocean_mask, kappa_sq, scale_field):
        args = (warm_start, probe_signs, ocean_mask, kappa_sq, scale_field)
        own, fields, to_odd, to_even = pl.pallas_call(
            functools.partial(pack_kernel, axes),
            out_shape=(
                f32(ROWS, FIELDS, LANES),
                f32(3, ROWS, LANES),
                f32(FIELDS, LANES),
                f32(FIELDS, LANES),
            ),
            in_specs=[pl.BlockSpec(memory_space=pltpu.HBM)] * 5,
            scratch_shapes=[pltpu.VMEM(x.shape, x.dtype) for x in args] + [pltpu.SemaphoreType.DMA((5,))],
            compiler_params=ALL_PARAMS,
            name="pack_edges",
        )(*args)
        odd_lat = exchanged(to_odd, lat, 1, False)
        even_lat = exchanged(to_even, lat, 0, False)
        to_odd, to_even = pl.pallas_call(
            functools.partial(send_kernel, axes),
            out_shape=(f32(SEND_ROWS, LANES), f32(SEND_ROWS, LANES)),
            compiler_params=PARAMS,
            name="pack_rows",
        )(own, fields, odd_lat, even_lat)
        odd_lon = exchanged(to_odd, lon, 1, True)
        even_lon = exchanged(to_even, lon, 0, True)
        inside = pl.pallas_call(
            functools.partial(inside_kernel, axes),
            out_shape=(f32(ROWS, FIELDS, 2 * LANES), f32(ROWS, 8, 2 * LANES))
            + (f32(ROWS, PROBES, 2 * LANES),) * len(HELD),
            compiler_params=PARAMS,
            cost_estimate=pl.CostEstimate(flops=40_000_000, bytes_accessed=8_000_000, transcendentals=0),
            name="inside_rows",
        )(own, odd_lat, even_lat)
        sums, basis, images, probe_image = pl.pallas_call(
            functools.partial(krylov_kernel, axes),
            out_shape=(
                f32(PROBES, LANES),
                f32(ROWS, 4 * PROBES, LANES),
                f32(ROWS, 4 * PROBES, LANES),
                f32(ROWS, PROBES, LANES),
            ),
            scratch_shapes=[
                pltpu.VMEM((TALL, FIELDS, 2 * LANES), jnp.float32),
                pltpu.VMEM((TALL, 8, 2 * LANES), jnp.float32),
            ]
            + [pltpu.VMEM((TALL, PROBES, 2 * LANES), jnp.float32)] * len(NEEDED),
            compiler_params=PARAMS,
            name="krylov_moments",
        )(*inside, odd_lon, even_lon)
        with jax.named_scope("sum_moments"):
            for group in stages:
                sums = spread_sum(sums, group)
        return pl.pallas_call(
            finish_kernel,
            out_shape=(
                f32(PROBES, ROWS, LANES),
                f32(PROBES, ROWS, LANES),
                f32(ROWS, LANES),
            ),
            scratch_shapes=[pltpu.VMEM((2 * PROBES, 4 * PROBES), jnp.float32)],
            compiler_params=PARAMS,
            name="solve_and_combine",
        )(sums, own, basis, images, probe_image)

    return local


def solution(mesh):
    if mesh.devices.shape == (16, 32):
        grid = Mesh(mesh.devices.reshape(2, 4, 2, 4, 8), ("zh", "x", "c", "zl", "y"))
        lat, lon = (("zh", "x", "c"), ("zl", "y"))
        stages = (("x", "c"), ("y",), ("zh", "zl"))
    else:
        grid, lat, lon, stages = (mesh, ("lat",), ("lon",), (("lat",), ("lon",)))
    return jax.shard_map(
        make_local(lat, lon, stages),
        mesh=grid,
        in_specs=(P(None, lon, lat), P(None, lon, lat), P(lon, lat), P(lon, lat), P(lon, lat)),
        out_specs=(P(None, lon, lat), P(None, lon, lat), P(lon, lat)),
        check_vma=False,
    )
```

```python
import functools

import jax
import jax.numpy as jnp
from jax import lax
from jax.experimental import pallas as pl
from jax.experimental.pallas import tpu as pltpu
from jax.sharding import Mesh
from jax.sharding import PartitionSpec as P

PROBES = 32
DEPTH = 8
ROWS = 16
LANES = 128
FIELDS = 72
SHIFT = 1.2
GAIN = 0.25
PARAMS = pltpu.CompilerParams(vmem_limit_bytes=32 * 1024 * 1024)


def parities(axes):
    return tuple(lax.rem(lax.axis_index(axis), 2) for axis in axes)


def pack_kernel(axes, warm_hbm, signs_hbm, mask_hbm, kappa_hbm, scale_hbm, own, fields, to_odd, to_even, *scratch):
    odd, _ = parities(axes)
    sems = scratch[-1]
    copies = [
        pltpu.make_async_copy(source, target, sems.at[n])
        for n, (source, target) in enumerate(
            zip((warm_hbm, signs_hbm, mask_hbm, kappa_hbm, scale_hbm), scratch[:-1], strict=True)
        )
    ]
    for copy in copies:
        copy.start()
    for copy in copies:
        copy.wait()
    warm, signs, mask, kappa, scale = scratch[:-1]
    wet = mask[...].astype(jnp.float32)
    diag = kappa[...] + 4.0
    scaled = scale[...]
    fields[0] = wet
    fields[1] = diag
    fields[2] = scaled
    block = lax.broadcasted_iota(jnp.int32, (FIELDS, LANES), 1) // DEPTH
    left_edge = jnp.zeros((FIELDS, LANES), jnp.float32)
    right_edge = jnp.zeros((FIELDS, LANES), jnp.float32)
    for i in range(ROWS):
        own[i, 0:PROBES, :] = warm[:, i, :]
        own[i, PROBES : 2 * PROBES, :] = 2.0 * signs[:, i, :].astype(jnp.float32) - 1.0
        own[i, 2 * PROBES :, :] = jnp.concatenate(
            [wet[i : i + 1], diag[i : i + 1], scaled[i : i + 1], jnp.zeros((5, LANES), jnp.float32)], axis=0
        )
        row = own[i]
        turned = pltpu.roll(row, DEPTH * i, 1) if i else row
        left_edge = jnp.where(block == i, turned, left_edge)
        right_edge = jnp.where(block == (i - 1) % ROWS, turned, right_edge)
    to_even[...] = jnp.where(odd == 0, right_edge, left_edge)
    to_odd[...] = jnp.where(odd == 0, left_edge, right_edge)


def sides(odd, even_side, odd_side):
    return jnp.where(odd == 0, odd_side, even_side), jnp.where(odd == 0, even_side, odd_side)


SEND_PROBES = DEPTH * PROBES
SEND_FIELDS = SEND_PROBES + (DEPTH - 2) * PROBES
SEND_CORNER = SEND_FIELDS + 3 * DEPTH
SEND_ROWS = SEND_CORNER + FIELDS


def send_kernel(axes, own, fields, from_odd, from_even, to_odd, to_even):
    odd_lat, odd_lon = parities(axes)
    lane = lax.broadcasted_iota(jnp.int32, (FIELDS, LANES), 1)
    before, after = sides(odd_lat, from_even[...], from_odd[...])
    first = jnp.where(lane < 64, after, pltpu.roll(before, 72, 1))
    last = jnp.where(lane < 64, pltpu.roll(after, 64, 1), pltpu.roll(before, 8, 1))
    for target, is_last in ((to_even, odd_lon == 0), (to_odd, odd_lon != 0)):
        start = jnp.where(is_last, DEPTH, 0)
        near = jnp.where(is_last, DEPTH + 2, 0)
        for j in range(DEPTH):
            target[j * PROBES : (j + 1) * PROBES, :] = own[start + j, 0:PROBES, :]
        for j in range(DEPTH - 2):
            target[SEND_PROBES + j * PROBES : SEND_PROBES + (j + 1) * PROBES, :] = own[near + j, PROBES : 2 * PROBES, :]
        for f in range(3):
            target[SEND_FIELDS + f * DEPTH : SEND_FIELDS + (f + 1) * DEPTH, :] = jnp.where(
                is_last, fields[f, DEPTH:, :], fields[f, 0:DEPTH, :]
            )
        target[SEND_CORNER:, :] = jnp.where(is_last, last, first)


TALL = ROWS + 2 * DEPTH
INSIDE = dict(mp=(8, 24), up=(9, 23), mw=(8, 24), i0=(9, 23), p0=(10, 22), m0=(10, 22), i1=(11, 21), p1=(12, 20), m1=(12, 20), i2=(13, 19), p2=(14, 18), m2=(14, 18), i3=(15, 17))
NEEDED = dict(mp=(7, 25), up=(8, 24), mw=(0, 32), i0=(1, 31), p0=(2, 30), m0=(2, 30), i1=(3, 29), p1=(4, 28), m1=(4, 28), i2=(5, 27), p2=(6, 26), m2=(6, 26), i3=(7, 25), p3=(8, 24))
HELD = tuple(INSIDE)


def fill_coef(coef, at, wet, diag, scaled):
    coef[at, 0:1, :] = wet
    coef[at, 1:2, :] = diag
    coef[at, 2:3, :] = wet * scaled
    coef[at, 3:4, :] = GAIN * wet
    coef[at, 4:5, :] = GAIN * ((1.0 - wet) - SHIFT)


def march(rows, coef, warm, probe, get, put):
    def stencil(name, r):
        here = get(name, r)
        around = get(name, r - 1) + get(name, r + 1)
        around = around + (pltpu.roll(here, 1, 1) + pltpu.roll(here, 2 * LANES - 1, 1))
        return coef(r, 1) * here - around

    for r in rows("mp"):
        put("mp", r, coef(r, 0) * probe(r))
    for r in rows("mw"):
        put("mw", r, coef(r, 0) * warm(r))
    for r in rows("i0"):
        put("i0", r, coef(r, 2) * stencil("mw", r))
    for r in rows("up"):
        put("up", r, coef(r, 2) * stencil("mp", r))
    for k in range(4):
        power = f"p{k}"
        for r in rows(power):
            if k == 0:
                value = probe(r) - (coef(r, 0) * stencil("i0", r) + (1.0 - coef(r, 0)) * warm(r))
            else:
                value = coef(r, 3) * stencil(f"i{k}", r) + coef(r, 4) * get(f"p{k - 1}", r)
            put(power, r, value)
            if k < 3:
                put(f"m{k}", r, coef(r, 0) * value)
        for r in rows(f"i{k + 1}"):
            put(f"i{k + 1}", r, coef(r, 2) * stencil(f"m{k}", r))


def inside_kernel(axes, own, from_odd, from_even, wide, coefs, *held):
    odd_lat, _ = parities(axes)
    held = dict(zip(HELD, held, strict=True))
    lane = lax.broadcasted_iota(jnp.int32, (FIELDS, LANES), 1)
    before, after = sides(odd_lat, from_even[...], from_odd[...])
    for i in range(ROWS):
        turn = (LANES - 8 * i) % LANES
        wide[i, :, 0:LANES] = own[i]
        wide[i, :, LANES:] = jnp.where(lane < 64, pltpu.roll(after, turn, 1), pltpu.roll(before, turn, 1))
        fill_coef(coefs, i, wide[i, 64:65, :], wide[i, 65:66, :], wide[i, 66:67, :])

    def put(name, r, value):
        held[name][r - DEPTH] = value

    march(
        lambda name: range(*INSIDE.get(name, (0, 0))),
        lambda r, n: coefs[r - DEPTH, n : n + 1, :],
        lambda r: wide[r - DEPTH, 0:PROBES, :],
        lambda r: wide[r - DEPTH, PROBES : 2 * PROBES, :],
        lambda name, r: held[name][r - DEPTH],
        put,
    )


def krylov_kernel(axes, own_wide, own_coefs, *refs):
    held = dict(zip(HELD, refs, strict=False))
    from_odd_lon, from_even_lon, sums, basis, images, probe_image, wide, coefs = refs[len(HELD) : len(HELD) + 8]
    fresh = dict(zip(NEEDED, refs[len(HELD) + 8 :], strict=True))
    _, odd_lon = parities(axes)
    lane = lax.broadcasted_iota(jnp.int32, (FIELDS, LANES), 1)
    for side, is_next in ((from_even_lon, odd_lon == 0), (from_odd_lon, odd_lon != 0)):
        start = jnp.where(is_next, DEPTH + ROWS, 0)
        near = jnp.where(is_next, DEPTH + ROWS, 2)
        pair = side[SEND_CORNER:, :]
        for j in range(DEPTH):
            wide[start + j, 0:PROBES, 0:LANES] = side[j * PROBES : (j + 1) * PROBES, :]
            for f in range(3):
                at = SEND_FIELDS + f * DEPTH + j
                wide[start + j, 2 * PROBES + f : 2 * PROBES + f + 1, 0:LANES] = side[at : at + 1, :]
            wide[start + j, :, LANES:] = jnp.where(
                lane < 64, pltpu.roll(pair, (LANES - 8 * j) % LANES, 1), pltpu.roll(pair, (56 - 8 * j) % LANES, 1)
            )
        for j in range(DEPTH - 2):
            at = SEND_PROBES + j * PROBES
            wide[near + j, PROBES : 2 * PROBES, 0:LANES] = side[at : at + PROBES, :]

    def own(r):
        return DEPTH <= r < DEPTH + ROWS

    for r in range(TALL):
        if not own(r):
            fill_coef(coefs, r, wide[r, 64:65, :], wide[r, 65:66, :], wide[r, 66:67, :])

    def rows(name):
        done = range(*INSIDE.get(name, (0, 0)))
        return [r for r in range(*NEEDED.get(name, (0, 0))) if r not in done]

    def get(name, r):
        return held[name][r - DEPTH] if r in range(*INSIDE.get(name, (0, 0))) else fresh[name][r]

    def put(name, r, value):
        fresh[name][r] = value

    def coef(r, n):
        return own_coefs[r - DEPTH, n : n + 1, :] if own(r) else coefs[r, n : n + 1, :]

    def argument(r, at):
        if own(r):
            return own_wide[r - DEPTH, at : at + PROBES, :]
        return wide[r, at : at + PROBES, :]

    march(rows, coef, lambda r: argument(r, 0), lambda r: argument(r, PROBES), get, put)

    total = jnp.zeros((3 * PROBES, 4 * PROBES), jnp.float32)
    for i in range(ROWS):
        r = DEPTH + i
        for k in range(4):
            at = slice(k * PROBES, (k + 1) * PROBES)
            basis[i, at, :] = get(f"p{k}", r)[:, 0:LANES]
            images[i, at, :] = get(f"i{(k + 1) % 4}", r)[:, 0:LANES]
        probe_image[i] = get("up", r)[:, 0:LANES]
        block = basis[i]
        total = total + lax.dot_general(
            block[0 : 3 * PROBES],
            block,
            (((1,), (1,)), ((), ())),
            precision=lax.Precision.HIGHEST,
            preferred_element_type=jnp.float32,
        )
    lane = lax.broadcasted_iota(jnp.int32, (PROBES, LANES), 1)
    row = lax.broadcasted_iota(jnp.int32, (PROBES, LANES), 0)
    packed = jnp.zeros((PROBES, LANES), jnp.float32)
    for b in range(3):
        even = total[b * PROBES : (b + 1) * PROBES]
        odd = pltpu.roll(even, LANES - PROBES, 1)
        column = lane - b * PROBES
        inside = (column >= 0) & (column < PROBES)
        packed = jnp.where(inside, jnp.where(column >= row, even, odd), packed)
        odd_diagonal = jnp.sum(jnp.where(column == row, odd, 0.0), axis=1, keepdims=True)
        packed = jnp.where(lane == 3 * PROBES + b, odd_diagonal, packed)
    sums[...] = packed


def dot(left, right, precision):
    return jnp.dot(left, right, precision=precision, preferred_element_type=jnp.float32)


def invert_pair(p):
    scale = 1.0 / (p[0][0] * p[1][1] - p[0][1] * p[0][1])
    return p[1][1] * scale, -p[0][1] * scale, p[0][0] * scale


def prepare(p):
    n = len(p)
    if n == 2:
        a, b, c = invert_pair(p)
        return lambda r: [a * r[0] + b * r[1], b * r[0] + c * r[1]]
    h = n // 2
    top = prepare([row[:h] for row in p[:h]])
    side = [row[h:] for row in p[:h]]
    solved = list(zip(*[top([side[i][j] for i in range(h)]) for j in range(h)], strict=True))

    def product(rows, weights):
        terms = [row * weight for row, weight in zip(rows, weights, strict=True)]
        while len(terms) > 1:
            terms = [sum(terms[i : i + 2][1:], terms[i]) for i in range(0, len(terms), 2)]
        return terms[0]

    rest = [[None] * h for _ in range(h)]
    for i in range(h):
        for j in range(i, h):
            rest[i][j] = p[h + i][h + j] - product([side[t][i] for t in range(h)], [solved[t][j] for t in range(h)])
            rest[j][i] = rest[i][j]
    bottom = prepare(rest)

    def solve(r):
        upper = top(r[:h])
        lower = bottom([r[h + i] - product([side[t][i] for t in range(h)], upper) for i in range(h)])
        return [upper[t] - product(solved[t], lower) for t in range(h)] + lower

    return solve


def eliminate(parts):
    row = lax.broadcasted_iota(jnp.int32, (8, LANES), 0)

    def spread(value):
        return jnp.broadcast_to(value, (8, LANES))

    for home in range(len(parts)):
        at = 8 * home
        columns = [[spread(part[:, at + j : at + j + 1]) for j in range(8)] for part in parts]
        pivot = [[spread(columns[home][j][i : i + 1]) for j in range(8)] for i in range(8)]
        solved = prepare(pivot)([spread(parts[home][i : i + 1]) for i in range(8)])
        for v, column in enumerate(columns):
            if v == home:
                part = solved[0]
                for i in range(1, 8):
                    part = jnp.where(row == i, solved[i], part)
                parts[v] = part
            else:
                terms = [c * x for c, x in zip(column, solved, strict=True)]
                parts[v] = parts[v] - (
                    ((terms[0] + terms[1]) + (terms[2] + terms[3])) + ((terms[4] + terms[5]) + (terms[6] + terms[7]))
                )
    return parts


def finish_kernel(
    sums, own, basis, images, probe_image,
    solution_out, residual_out, grad_out,
    coeffs,
):
    packed = sums[...]
    flipped = packed.T
    lane = lax.broadcasted_iota(jnp.int32, (PROBES, PROBES), 1)
    row = lax.broadcasted_iota(jnp.int32, (PROBES, PROBES), 0)
    moments = []
    for b in range(3):
        block = packed[:, b * PROBES : (b + 1) * PROBES]
        mirror = flipped[b * PROBES : (b + 1) * PROBES, :]
        moments.append(jnp.where(lane >= row, block, mirror))
        odd = jnp.where(lane < row, block, mirror)
        moments.append(jnp.where(lane == row, packed[:, 3 * PROBES + b : 3 * PROBES + b + 1], odd))
    power = [moments[k + 1] * (1.0 / GAIN) + moments[k] * SHIFT for k in range(5)]

    table = jnp.concatenate(
        [jnp.concatenate([power[b], power[b + 1], power[b + 2], moments[b]], axis=1) for b in range(3)], axis=0
    )
    parts = eliminate([table[8 * v : 8 * v + 8] for v in range(12)])
    solved = jnp.concatenate(parts, axis=0)

    nothing = jnp.zeros((PROBES, LANES), jnp.float32)
    wide_lane = lax.broadcasted_iota(jnp.int32, (4 * PROBES, LANES), 1)
    wide_row = lax.broadcasted_iota(jnp.int32, (4 * PROBES, LANES), 0)
    one = (wide_lane == wide_row + 3 * PROBES).astype(jnp.float32)
    kept = jnp.concatenate([solved, nothing], axis=0)
    left = one - SHIFT * kept - (1.0 / GAIN) * jnp.concatenate([nothing, solved], axis=0)
    columns = jnp.where(wide_lane < PROBES, pltpu.roll(kept, PROBES, 1), pltpu.roll(left, 2 * PROBES, 1))
    coeffs[...] = columns.T[0 : 2 * PROBES]
    weights = coeffs[0:PROBES, :] + one[0:PROBES]

    for i in range(ROWS):
        both = dot(coeffs[...], basis[i], lax.Precision.HIGHEST)
        values = both[0:PROBES] + own[i, 0:PROBES, :]
        solution_out[:, i, :] = values
        residual_out[:, i, :] = both[PROBES:]
        image = dot(weights, images[i], lax.Precision.HIGH)
        terms = values * probe_image[i] + image * own[i, PROBES : 2 * PROBES, :]
        wet = own[i, 64:65, :]
        grad_out[i : i + 1, :] = wet * (jnp.sum(terms, axis=0, keepdims=True) * (1.0 / PROBES))


def f32(*shape):
    return jax.ShapeDtypeStruct(shape, jnp.float32)


def exchanged(value, axes, odd, wrap):
    size = lax.axis_size(axes)
    pairs = []
    for i in range(size):
        other = ((i + odd) ^ 1) - odd
        if wrap or 0 <= other < size:
            pairs.append((i, other % size))
    return lax.ppermute(value, axes, pairs)


def spread_sum(value, axes):
    size = lax.axis_size(axes)
    copies = jnp.broadcast_to(value[None], (size,) + value.shape)
    return jnp.sum(lax.all_to_all(copies, axes, 0, 0), axis=0)


def make_local(lat, lon, stages):
    axes = (lat[-1], lon[-1])

    def local(warm_start, probe_signs, ocean_mask, kappa_sq, scale_field):
        args = (warm_start, probe_signs, ocean_mask, kappa_sq, scale_field)
        own, fields, to_odd, to_even = pl.pallas_call(
            functools.partial(pack_kernel, axes),
            out_shape=(
                f32(ROWS, FIELDS, LANES),
                f32(3, ROWS, LANES),
                f32(FIELDS, LANES),
                f32(FIELDS, LANES),
            ),
            in_specs=[pl.BlockSpec(memory_space=pltpu.HBM)] * 5,
            scratch_shapes=[pltpu.VMEM(x.shape, x.dtype) for x in args] + [pltpu.SemaphoreType.DMA((5,))],
            compiler_params=PARAMS,
            name="pack_edges",
        )(*(pltpu.with_memory_space_constraint(x, pltpu.HBM) for x in args))
        odd_lat = exchanged(to_odd, lat, 1, False)
        even_lat = exchanged(to_even, lat, 0, False)
        to_odd, to_even = pl.pallas_call(
            functools.partial(send_kernel, axes),
            out_shape=(f32(SEND_ROWS, LANES), f32(SEND_ROWS, LANES)),
            compiler_params=PARAMS,
            name="pack_rows",
        )(own, fields, odd_lat, even_lat)
        odd_lon = exchanged(to_odd, lon, 1, True)
        even_lon = exchanged(to_even, lon, 0, True)
        inside = pl.pallas_call(
            functools.partial(inside_kernel, axes),
            out_shape=(f32(ROWS, FIELDS, 2 * LANES), f32(ROWS, 8, 2 * LANES))
            + (f32(ROWS, PROBES, 2 * LANES),) * len(HELD),
            compiler_params=PARAMS,
            cost_estimate=pl.CostEstimate(flops=40_000_000, bytes_accessed=8_000_000, transcendentals=0),
            name="inside_rows",
        )(own, odd_lat, even_lat)
        sums, basis, images, probe_image = pl.pallas_call(
            functools.partial(krylov_kernel, axes),
            out_shape=(
                f32(PROBES, LANES),
                f32(ROWS, 4 * PROBES, LANES),
                f32(ROWS, 4 * PROBES, LANES),
                f32(ROWS, PROBES, LANES),
            ),
            scratch_shapes=[
                pltpu.VMEM((TALL, FIELDS, 2 * LANES), jnp.float32),
                pltpu.VMEM((TALL, 8, 2 * LANES), jnp.float32),
            ]
            + [pltpu.VMEM((TALL, PROBES, 2 * LANES), jnp.float32)] * len(NEEDED),
            compiler_params=PARAMS,
            name="krylov_moments",
        )(*inside, odd_lon, even_lon)
        with jax.named_scope("sum_moments"):
            for group in stages:
                sums = spread_sum(sums, group)
        return pl.pallas_call(
            finish_kernel,
            out_shape=(
                f32(PROBES, ROWS, LANES),
                f32(PROBES, ROWS, LANES),
                f32(ROWS, LANES),
            ),
            scratch_shapes=[pltpu.VMEM((2 * PROBES, 4 * PROBES), jnp.float32)],
            compiler_params=PARAMS,
            name="solve_and_combine",
        )(sums, own, basis, images, probe_image)

    return local


def solution(mesh):
    if mesh.devices.shape == (16, 32):
        grid = Mesh(mesh.devices.reshape(2, 4, 2, 4, 8), ("zh", "x", "c", "zl", "y"))
        lat, lon = (("zh", "x", "c"), ("zl", "y"))
        stages = (("x", "c"), ("y",), ("zh", "zl"))
    else:
        grid, lat, lon, stages = (mesh, ("lat",), ("lon",), (("lat",), ("lon",)))
    return jax.shard_map(
        make_local(lat, lon, stages),
        mesh=grid,
        in_specs=(P(None, lon, lat), P(None, lon, lat), P(lon, lat), P(lon, lat), P(lon, lat)),
        out_specs=(P(None, lon, lat), P(None, lon, lat), P(lon, lat)),
        check_vma=False,
    )
```

```python
import functools

import jax
import jax.numpy as jnp
from jax import lax
from jax.experimental import pallas as pl
from jax.experimental.pallas import tpu as pltpu
from jax.sharding import Mesh
from jax.sharding import PartitionSpec as P

PROBES = 32
DEPTH = 8
ROWS = 16
LANES = 128
FIELDS = 72
SHIFT = 1.2
GAIN = 0.25
PARAMS = pltpu.CompilerParams(vmem_limit_bytes=32 * 1024 * 1024)


def parities(axes):
    return tuple(lax.rem(lax.axis_index(axis), 2) for axis in axes)


def pack_kernel(axes, warm_hbm, signs_hbm, mask_hbm, kappa_hbm, scale_hbm, own, fields, to_odd, to_even, *scratch):
    odd, odd_lon = parities(axes)
    sems = scratch[-1]
    copies = [
        pltpu.make_async_copy(source, target, sems.at[n])
        for n, (source, target) in enumerate(
            zip((warm_hbm, signs_hbm, mask_hbm, kappa_hbm, scale_hbm), scratch[:-1], strict=True)
        )
    ]
    for copy in copies:
        copy.start()
    for copy in copies:
        copy.wait()
    warm, signs, mask, kappa, scale = scratch[:-1]
    wet = mask[...].astype(jnp.float32)
    diag = kappa[...] + 4.0
    scaled = scale[...]
    for p in range(ROWS):
        row = own.at[jnp.where(odd_lon == 0, p, ROWS - 1 - p)]
        row[0:PROBES, :] = warm[:, p, :]
        row[PROBES : 2 * PROBES, :] = 2.0 * signs[:, p, :].astype(jnp.float32) - 1.0
        row[2 * PROBES :, :] = jnp.concatenate(
            [wet[p : p + 1], diag[p : p + 1], scaled[p : p + 1], jnp.zeros((5, LANES), jnp.float32)], axis=0
        )
    block = lax.broadcasted_iota(jnp.int32, (FIELDS, LANES), 1) // DEPTH
    left_edge = jnp.zeros((FIELDS, LANES), jnp.float32)
    right_edge = jnp.zeros((FIELDS, LANES), jnp.float32)
    for i in range(ROWS):
        row = own[i]
        for f in range(3):
            fields[f, i : i + 1, :] = row[2 * PROBES + f : 2 * PROBES + f + 1]
        turned = pltpu.roll(row, DEPTH * i, 1) if i else row
        left_edge = jnp.where(block == i, turned, left_edge)
        right_edge = jnp.where(block == (i - 1) % ROWS, turned, right_edge)
    to_even[...] = jnp.where(odd == 0, right_edge, left_edge)
    to_odd[...] = jnp.where(odd == 0, left_edge, right_edge)


def sides(odd, even_side, odd_side):
    return jnp.where(odd == 0, odd_side, even_side), jnp.where(odd == 0, even_side, odd_side)


SEND_PROBES = DEPTH * PROBES
SEND_FIELDS = SEND_PROBES + (DEPTH - 2) * PROBES
SEND_CORNER = SEND_FIELDS + 3 * DEPTH
SEND_ROWS = SEND_CORNER + FIELDS


def send_kernel(axes, own, fields, from_odd, from_even, to_odd, to_even):
    odd_lat, _ = parities(axes)
    lane = lax.broadcasted_iota(jnp.int32, (FIELDS, LANES), 1)
    before, after = sides(odd_lat, from_even[...], from_odd[...])
    first = jnp.where(lane < 64, after, pltpu.roll(before, 72, 1))
    last = jnp.where(lane < 64, pltpu.roll(after, 64, 1), pltpu.roll(before, 8, 1))
    for target, corner, low, row in (
        (to_odd, first, 0, lambda j: j),
        (to_even, last, DEPTH, lambda j: ROWS - 1 - j),
    ):
        for j in range(DEPTH):
            target[j * PROBES : (j + 1) * PROBES, :] = own[row(j), 0:PROBES, :]
        for j in range(DEPTH - 2):
            target[SEND_PROBES + j * PROBES : SEND_PROBES + (j + 1) * PROBES, :] = own[row(j), PROBES : 2 * PROBES, :]
        for f in range(3):
            target[SEND_FIELDS + f * DEPTH : SEND_FIELDS + (f + 1) * DEPTH, :] = fields[f, low : low + DEPTH, :]
        target[SEND_CORNER:, :] = corner


TALL = ROWS + 2 * DEPTH
INSIDE = dict(mp=(8, 24), up=(9, 23), mw=(8, 24), i0=(9, 23), p0=(10, 22), m0=(10, 22), i1=(11, 21), p1=(12, 20), m1=(12, 20), i2=(13, 19), p2=(14, 18), m2=(14, 18), i3=(15, 17), p3=(16, 16))
NEEDED = dict(mp=(7, 25), up=(8, 24), mw=(0, 32), i0=(1, 31), p0=(2, 30), m0=(2, 30), i1=(3, 29), p1=(4, 28), m1=(4, 28), i2=(5, 27), p2=(6, 26), m2=(6, 26), i3=(7, 25), p3=(8, 24))
HELD = tuple(name for name in INSIDE if name != "p3")
HALF = ROWS // 2


def fill_coef(coef, at, wet, diag, scaled):
    coef[at, 0:1, :] = wet
    coef[at, 1:2, :] = diag
    coef[at, 2:3, :] = wet * scaled
    coef[at, 3:4, :] = GAIN * wet
    coef[at, 4:5, :] = GAIN * ((1.0 - wet) - SHIFT)


def march(rows, coef, warm, probe, get, put):
    def stencil(name, r):
        here = get(name, r)
        around = get(name, r - 1) + get(name, r + 1)
        around = around + (pltpu.roll(here, 1, 1) + pltpu.roll(here, 2 * LANES - 1, 1))
        return coef(r, 1) * here - around

    for r in rows("mp"):
        put("mp", r, coef(r, 0) * probe(r))
    for r in rows("mw"):
        put("mw", r, coef(r, 0) * warm(r))
    for r in rows("i0"):
        put("i0", r, coef(r, 2) * stencil("mw", r))
    for r in rows("up"):
        put("up", r, coef(r, 2) * stencil("mp", r))
    for k in range(4):
        power = f"p{k}"
        for r in rows(power):
            if k == 0:
                value = probe(r) - (coef(r, 0) * stencil("i0", r) + (1.0 - coef(r, 0)) * warm(r))
            else:
                value = coef(r, 3) * stencil(f"i{k}", r) + coef(r, 4) * get(f"p{k - 1}", r)
            put(power, r, value)
            if k < 3:
                put(f"m{k}", r, coef(r, 0) * value)
        for r in rows(f"i{k + 1}"):
            put(f"i{k + 1}", r, coef(r, 2) * stencil(f"m{k}", r))


def inside_kernel(axes, own, from_odd, from_even, wide, coefs, *held):
    odd_lat, _ = parities(axes)
    held = dict(zip(HELD, held, strict=True))
    lane = lax.broadcasted_iota(jnp.int32, (FIELDS, LANES), 1)
    before, after = sides(odd_lat, from_even[...], from_odd[...])
    for i in range(ROWS):
        turn = (LANES - 8 * i) % LANES
        wide[i, :, 0:LANES] = own[i]
        wide[i, :, LANES:] = jnp.where(lane < 64, pltpu.roll(after, turn, 1), pltpu.roll(before, turn, 1))
        fill_coef(coefs, i, wide[i, 64:65, :], wide[i, 65:66, :], wide[i, 66:67, :])

    def put(name, r, value):
        held[name][r - DEPTH] = value

    march(
        lambda name: range(*INSIDE.get(name, (0, 0))),
        lambda r, n: coefs[r - DEPTH, n : n + 1, :],
        lambda r: wide[r - DEPTH, 0:PROBES, :],
        lambda r: wide[r - DEPTH, PROBES : 2 * PROBES, :],
        lambda name, r: held[name][r - DEPTH],
        put,
    )


def half_kernel(behind, own_wide, own_coefs, *refs):
    held = dict(zip(HELD, refs, strict=False))
    refs = refs[len(HELD) :]
    if behind:
        other, message, sums, basis, images, probe_image, wide, coefs, *fresh = refs
    else:
        message, sums, basis, images, probe_image, wide, coefs, *fresh = refs
    fresh = dict(zip(NEEDED, fresh, strict=True))
    lane = lax.broadcasted_iota(jnp.int32, (FIELDS, LANES), 1)
    pair = message[SEND_CORNER:, :]
    for j in range(DEPTH):
        place = DEPTH - 1 - j if behind else j
        wide[j, 0:PROBES, 0:LANES] = message[j * PROBES : (j + 1) * PROBES, :]
        if j < DEPTH - 2:
            at = SEND_PROBES + j * PROBES
            wide[j, PROBES : 2 * PROBES, 0:LANES] = message[at : at + PROBES, :]
        for f in range(3):
            at = SEND_FIELDS + f * DEPTH + place
            wide[j, 2 * PROBES + f : 2 * PROBES + f + 1, 0:LANES] = message[at : at + 1, :]
        after = pltpu.roll(pair, (LANES - 8 * place) % LANES, 1)
        before = pltpu.roll(pair, (56 - 8 * place) % LANES, 1)
        wide[j, :, LANES:] = jnp.where(lane < 64, after, before)
        fill_coef(coefs, j, wide[j, 64:65, :], wide[j, 65:66, :], wide[j, 66:67, :])

    base = TALL // 2 if behind else 0

    def own(r):
        return DEPTH <= r < DEPTH + ROWS

    def halo(r):
        return r - (DEPTH + ROWS) if behind else DEPTH - 1 - r

    def rows(name):
        if name not in NEEDED:
            return range(0)
        return range(INSIDE[name][1], NEEDED[name][1]) if behind else range(NEEDED[name][0], INSIDE[name][0])

    def get(name, r):
        return fresh[name][r - base] if r in rows(name) else held[name][r - DEPTH]

    def put(name, r, value):
        fresh[name][r - base] = value

    def coef(r, n):
        return own_coefs[r - DEPTH, n : n + 1, :] if own(r) else coefs[halo(r), n : n + 1, :]

    def argument(r, at):
        return own_wide[r - DEPTH, at : at + PROBES, :] if own(r) else wide[halo(r), at : at + PROBES, :]

    march(rows, coef, lambda r: argument(r, 0), lambda r: argument(r, PROBES), get, put)

    total = other[...] if behind else jnp.zeros((3 * PROBES, 4 * PROBES), jnp.float32)
    for i in range(HALF):
        r = DEPTH + i + (HALF if behind else 0)
        for k in range(4):
            at = slice(k * PROBES, (k + 1) * PROBES)
            basis[i, at, :] = get(f"p{k}", r)[:, 0:LANES]
            images[i, at, :] = get(f"i{(k + 1) % 4}", r)[:, 0:LANES]
        probe_image[i] = get("up", r)[:, 0:LANES]
        block = basis[i]
        total = total + lax.dot_general(
            block[0 : 3 * PROBES],
            block,
            (((1,), (1,)), ((), ())),
            precision=lax.Precision.HIGHEST,
            preferred_element_type=jnp.float32,
        )
    if not behind:
        sums[...] = total
        return
    lane = lax.broadcasted_iota(jnp.int32, (PROBES, LANES), 1)
    row = lax.broadcasted_iota(jnp.int32, (PROBES, LANES), 0)
    packed = jnp.zeros((PROBES, LANES), jnp.float32)
    for b in range(3):
        even = total[b * PROBES : (b + 1) * PROBES]
        odd = pltpu.roll(even, LANES - PROBES, 1)
        column = lane - b * PROBES
        inside = (column >= 0) & (column < PROBES)
        packed = jnp.where(inside, jnp.where(column >= row, even, odd), packed)
        odd_diagonal = jnp.sum(jnp.where(column == row, odd, 0.0), axis=1, keepdims=True)
        packed = jnp.where(lane == 3 * PROBES + b, odd_diagonal, packed)
    sums[...] = packed


def dot(left, right, precision):
    return jnp.dot(left, right, precision=precision, preferred_element_type=jnp.float32)


def invert_pair(p):
    scale = 1.0 / (p[0][0] * p[1][1] - p[0][1] * p[0][1])
    return p[1][1] * scale, -p[0][1] * scale, p[0][0] * scale


def prepare(p):
    n = len(p)
    if n == 2:
        a, b, c = invert_pair(p)
        return lambda r: [a * r[0] + b * r[1], b * r[0] + c * r[1]]
    h = n // 2
    top = prepare([row[:h] for row in p[:h]])
    side = [row[h:] for row in p[:h]]
    solved = list(zip(*[top([side[i][j] for i in range(h)]) for j in range(h)], strict=True))

    def product(rows, weights):
        terms = [row * weight for row, weight in zip(rows, weights, strict=True)]
        while len(terms) > 1:
            terms = [sum(terms[i : i + 2][1:], terms[i]) for i in range(0, len(terms), 2)]
        return terms[0]

    rest = [[None] * h for _ in range(h)]
    for i in range(h):
        for j in range(i, h):
            rest[i][j] = p[h + i][h + j] - product([side[t][i] for t in range(h)], [solved[t][j] for t in range(h)])
            rest[j][i] = rest[i][j]
    bottom = prepare(rest)

    def solve(r):
        upper = top(r[:h])
        lower = bottom([r[h + i] - product([side[t][i] for t in range(h)], upper) for i in range(h)])
        return [upper[t] - product(solved[t], lower) for t in range(h)] + lower

    return solve


def eliminate(parts):
    row = lax.broadcasted_iota(jnp.int32, (8, LANES), 0)

    def spread(value):
        return jnp.broadcast_to(value, (8, LANES))

    def take(part, lane):
        return jnp.take_along_axis(part, jnp.full((8, LANES), lane, jnp.int32), axis=1)

    for home in range(len(parts)):
        at = 8 * home
        column = [take(parts[home], at + j) for j in range(8)]
        pivot = [[spread(column[j][i : i + 1]) for j in range(8)] for i in range(8)]
        solved = prepare(pivot)([spread(parts[home][i : i + 1]) for i in range(8)])
        for v in [*range(home, len(parts)), *range(home)]:
            if v == home:
                part = solved[0]
                for i in range(1, 8):
                    part = jnp.where(row == i, solved[i], part)
                parts[v] = part
            else:
                terms = [take(parts[v], at + j) * solved[j] for j in range(8)]
                parts[v] = parts[v] - (
                    ((terms[0] + terms[1]) + (terms[2] + terms[3])) + ((terms[4] + terms[5]) + (terms[6] + terms[7]))
                )
    return parts


def finish_kernel(
    axes,
    sums, own, basis_first, basis_last, images_first, images_last, probe_first, probe_last,
    solution_out, residual_out, grad_out,
    coeffs, rows,
):
    _, odd_lon = parities(axes)
    packed = sums[...]
    flipped = packed.T
    lane = lax.broadcasted_iota(jnp.int32, (PROBES, PROBES), 1)
    row = lax.broadcasted_iota(jnp.int32, (PROBES, PROBES), 0)
    moments = []
    for b in range(3):
        block = packed[:, b * PROBES : (b + 1) * PROBES]
        mirror = flipped[b * PROBES : (b + 1) * PROBES, :]
        moments.append(jnp.where(lane >= row, block, mirror))
        odd = jnp.where(lane < row, block, mirror)
        moments.append(jnp.where(lane == row, packed[:, 3 * PROBES + b : 3 * PROBES + b + 1], odd))
    power = [moments[k + 1] * (1.0 / GAIN) + moments[k] * SHIFT for k in range(5)]

    table = jnp.concatenate(
        [jnp.concatenate([power[b], power[b + 1], power[b + 2], moments[b]], axis=1) for b in range(3)], axis=0
    )
    parts = eliminate([table[8 * v : 8 * v + 8] for v in range(12)])
    solved = jnp.concatenate(parts, axis=0)

    t = [jnp.sum(jnp.where(lane == row, m, 0.0), axis=(0, 1), keepdims=True) for m in moments]
    a = t[1] / t[0]
    n1 = t[2] - a * t[1]
    b0, b1 = (t[2] / t[0], (t[3] - a * t[2]) / n1)
    b2 = b1 * a - b0
    c0, c1 = (t[3] / t[0], (t[4] - a * t[3]) / n1)
    c2 = (t[5] - b1 * t[4] + b2 * t[3]) / (t[4] - b1 * t[3] + b2 * t[2])

    nothing = jnp.zeros((PROBES, LANES), jnp.float32)
    wide_lane = lax.broadcasted_iota(jnp.int32, (4 * PROBES, LANES), 1)
    wide_row = lax.broadcasted_iota(jnp.int32, (4 * PROBES, LANES), 0)
    one = (wide_lane == wide_row + 3 * PROBES).astype(jnp.float32)
    kept = jnp.concatenate([solved, nothing], axis=0)
    left = one - SHIFT * kept - (1.0 / GAIN) * jnp.concatenate([nothing, solved], axis=0)

    def for_polynomials(v):
        v = [v[k * PROBES : (k + 1) * PROBES] for k in range(4)]
        return jnp.concatenate(
            [v[0] + a * v[1] + b0 * v[2] + c0 * v[3], v[1] + b1 * v[2] + c1 * v[3], v[2] + c2 * v[3], v[3]], axis=0
        )

    columns = jnp.where(
        wide_lane < PROBES,
        pltpu.roll(for_polynomials(kept), PROBES, 1),
        jnp.where(wide_lane < 2 * PROBES, pltpu.roll(for_polynomials(left), 2 * PROBES, 1), pltpu.roll(kept, 3 * PROBES, 1)),
    )
    coeffs[...] = columns.T[0 : 3 * PROBES]
    weights = coeffs[2 * PROBES :, :] + one[0:PROBES]
    a, b0, b1, c0, c1, c2 = (jnp.broadcast_to(x, (PROBES, LANES)) for x in (a, b0, b1, c0, c1, c2))

    for i in range(ROWS):
        j = i % HALF
        basis, images, probe_image = (
            (basis_first, images_first, probe_first) if i < HALF else (basis_last, images_last, probe_last)
        )
        v0 = basis[j, 0:PROBES, :]
        w1 = basis[j, PROBES : 2 * PROBES, :] - a * v0
        w2 = basis[j, 2 * PROBES : 3 * PROBES, :] - b1 * w1 - b0 * v0
        w3 = basis[j, 3 * PROBES :, :] - c2 * w2 - c1 * w1 - c0 * v0
        both = dot(coeffs[0 : 2 * PROBES, :], jnp.concatenate([v0, w1, w2, w3], axis=0), lax.Precision.HIGH)
        values = both[0:PROBES] + own[i, 0:PROBES, :]
        image = dot(weights, images[j], lax.Precision.HIGH)
        terms = values * probe_image[j] + image * own[i, PROBES : 2 * PROBES, :]
        wet = own[i, 64:65, :]
        out = rows.at[jnp.where(odd_lon == 0, i, ROWS - 1 - i)]
        out[0:PROBES, :] = values
        out[PROBES : 2 * PROBES, :] = both[PROBES:]
        out[2 * PROBES : 2 * PROBES + 1, :] = wet * (jnp.sum(terms, axis=0, keepdims=True) * (1.0 / PROBES))
    for p in range(ROWS):
        solution_out[:, p, :] = rows[p, 0:PROBES, :]
        residual_out[:, p, :] = rows[p, PROBES : 2 * PROBES, :]
        grad_out[p : p + 1, :] = rows[p, 2 * PROBES : 2 * PROBES + 1, :]


def f32(*shape):
    return jax.ShapeDtypeStruct(shape, jnp.float32)


def exchanged(value, axes, odd, wrap):
    size = lax.axis_size(axes)
    pairs = []
    for i in range(size):
        other = ((i + odd) ^ 1) - odd
        if wrap or 0 <= other < size:
            pairs.append((i, other % size))
    return lax.ppermute(value, axes, pairs)


def spread_sum(value, axes):
    size = lax.axis_size(axes)
    copies = jnp.broadcast_to(value[None], (size,) + value.shape)
    return jnp.sum(lax.all_to_all(copies, axes, 0, 0), axis=0)


def make_local(lat, lon, stages):
    axes = (lat[-1], lon[-1])

    def local(warm_start, probe_signs, ocean_mask, kappa_sq, scale_field):
        args = (warm_start, probe_signs, ocean_mask, kappa_sq, scale_field)
        own, fields, to_odd, to_even = pl.pallas_call(
            functools.partial(pack_kernel, axes),
            out_shape=(
                f32(ROWS, FIELDS, LANES),
                f32(3, ROWS, LANES),
                f32(FIELDS, LANES),
                f32(FIELDS, LANES),
            ),
            in_specs=[pl.BlockSpec(memory_space=pltpu.HBM)] * 5,
            scratch_shapes=[pltpu.VMEM(x.shape, x.dtype) for x in args] + [pltpu.SemaphoreType.DMA((5,))],
            compiler_params=PARAMS,
            name="pack_edges",
        )(*(pltpu.with_memory_space_constraint(x, pltpu.HBM) for x in args))
        odd_lat = exchanged(to_odd, lat, 1, False)
        even_lat = exchanged(to_even, lat, 0, False)
        to_odd, to_even = pl.pallas_call(
            functools.partial(send_kernel, axes),
            out_shape=(f32(SEND_ROWS, LANES), f32(SEND_ROWS, LANES)),
            compiler_params=PARAMS,
            name="pack_rows",
        )(own, fields, odd_lat, even_lat)
        odd_lon = exchanged(to_odd, lon, 1, True)
        even_lon = exchanged(to_even, lon, 0, True)
        inside = pl.pallas_call(
            functools.partial(inside_kernel, axes),
            out_shape=(f32(ROWS, FIELDS, 2 * LANES), f32(ROWS, 8, 2 * LANES))
            + (f32(ROWS, PROBES, 2 * LANES),) * len(HELD),
            compiler_params=PARAMS,
            cost_estimate=pl.CostEstimate(flops=40_000_000, bytes_accessed=8_000_000, transcendentals=0),
            name="inside_rows",
        )(own, odd_lat, even_lat)
        half = dict(
            scratch_shapes=[
                pltpu.VMEM((DEPTH, FIELDS, 2 * LANES), jnp.float32),
                pltpu.VMEM((DEPTH, 8, 2 * LANES), jnp.float32),
            ]
            + [pltpu.VMEM((TALL // 2, PROBES, 2 * LANES), jnp.float32)] * len(NEEDED),
            compiler_params=PARAMS,
            cost_estimate=pl.CostEstimate(flops=40_000_000, bytes_accessed=8_000_000, transcendentals=0),
        )
        filled = (f32(HALF, 4 * PROBES, LANES), f32(HALF, 4 * PROBES, LANES), f32(HALF, PROBES, LANES))
        part, *first = pl.pallas_call(
            functools.partial(half_kernel, False),
            out_shape=(f32(3 * PROBES, LANES), *filled),
            name="first_rows",
            **half,
        )(*inside, odd_lon)
        sums, *last = pl.pallas_call(
            functools.partial(half_kernel, True),
            out_shape=(f32(PROBES, LANES), *filled),
            name="last_rows",
            **half,
        )(*inside, part, even_lon)
        with jax.named_scope("sum_moments"):
            for group in stages:
                sums = spread_sum(sums, group)
        return pl.pallas_call(
            functools.partial(finish_kernel, axes),
            out_shape=(
                f32(PROBES, ROWS, LANES),
                f32(PROBES, ROWS, LANES),
                f32(ROWS, LANES),
            ),
            scratch_shapes=[
                pltpu.VMEM((3 * PROBES, 4 * PROBES), jnp.float32),
                pltpu.VMEM((ROWS, FIELDS, LANES), jnp.float32),
            ],
            compiler_params=PARAMS,
            name="solve_and_combine",
        )(sums, own, *(x for pair in zip(first, last, strict=True) for x in pair))

    return local


def solution(mesh):
    if mesh.devices.shape == (16, 32):
        grid = Mesh(mesh.devices.reshape(2, 4, 2, 4, 8), ("zh", "x", "c", "zl", "y"))
        lat, lon = (("zh", "x", "c"), ("zl", "y"))
        stages = (("x", "c"), ("y",), ("zh", "zl"))
    else:
        grid, lat, lon, stages = (mesh, ("lat",), ("lon",), (("lat",), ("lon",)))
    return jax.shard_map(
        make_local(lat, lon, stages),
        mesh=grid,
        in_specs=(P(None, lon, lat), P(None, lon, lat), P(lon, lat), P(lon, lat), P(lon, lat)),
        out_specs=(P(None, lon, lat), P(None, lon, lat), P(lon, lat)),
        check_vma=False,
    )
```

```python
import functools

import jax
import jax.numpy as jnp
from jax import lax
from jax.experimental import pallas as pl
from jax.experimental.pallas import tpu as pltpu
from jax.sharding import Mesh
from jax.sharding import PartitionSpec as P

PROBES = 32
DEPTH = 8
ROWS = 16
LANES = 128
FIELDS = 72
SHIFT = 1.2
GAIN = 0.25
PARAMS = pltpu.CompilerParams(vmem_limit_bytes=32 * 1024 * 1024)


def parities(axes):
    return tuple(lax.rem(lax.axis_index(axis), 2) for axis in axes)


def pack_kernel(axes, warm_hbm, signs_hbm, mask_hbm, kappa_hbm, scale_hbm, own, fields, to_odd, to_even, *scratch):
    odd, odd_lon = parities(axes)
    sems = scratch[-1]
    copies = [
        pltpu.make_async_copy(source, target, sems.at[n])
        for n, (source, target) in enumerate(
            zip((warm_hbm, signs_hbm, mask_hbm, kappa_hbm, scale_hbm), scratch[:-1], strict=True)
        )
    ]
    for copy in copies:
        copy.start()
    for copy in copies:
        copy.wait()
    warm, signs, mask, kappa, scale = scratch[:-1]
    wet = mask[...].astype(jnp.float32)
    diag = kappa[...] + 4.0
    scaled = scale[...]
    for p in range(ROWS):
        row = own.at[jnp.where(odd_lon == 0, p, ROWS - 1 - p)]
        row[0:PROBES, :] = warm[:, p, :]
        row[PROBES : 2 * PROBES, :] = 2.0 * signs[:, p, :].astype(jnp.float32) - 1.0
        row[2 * PROBES :, :] = jnp.concatenate(
            [wet[p : p + 1], diag[p : p + 1], scaled[p : p + 1], jnp.zeros((5, LANES), jnp.float32)], axis=0
        )
    block = lax.broadcasted_iota(jnp.int32, (FIELDS, LANES), 1) // DEPTH
    left_edge = jnp.zeros((FIELDS, LANES), jnp.float32)
    right_edge = jnp.zeros((FIELDS, LANES), jnp.float32)
    for i in range(ROWS):
        row = own[i]
        for f in range(3):
            fields[f, i : i + 1, :] = row[2 * PROBES + f : 2 * PROBES + f + 1]
        turned = pltpu.roll(row, DEPTH * i, 1) if i else row
        left_edge = jnp.where(block == i, turned, left_edge)
        right_edge = jnp.where(block == (i - 1) % ROWS, turned, right_edge)
    to_even[...] = jnp.where(odd == 0, right_edge, left_edge)
    to_odd[...] = jnp.where(odd == 0, left_edge, right_edge)


def sides(odd, even_side, odd_side):
    return jnp.where(odd == 0, odd_side, even_side), jnp.where(odd == 0, even_side, odd_side)


SEND_PROBES = DEPTH * PROBES
SEND_FIELDS = SEND_PROBES + (DEPTH - 2) * PROBES
SEND_CORNER = SEND_FIELDS + 3 * DEPTH
SEND_ROWS = SEND_CORNER + FIELDS


def send_kernel(axes, own, fields, from_odd, from_even, to_odd, to_even):
    odd_lat, _ = parities(axes)
    lane = lax.broadcasted_iota(jnp.int32, (FIELDS, LANES), 1)
    before, after = sides(odd_lat, from_even[...], from_odd[...])
    first = jnp.where(lane < 64, after, pltpu.roll(before, 72, 1))
    last = jnp.where(lane < 64, pltpu.roll(after, 64, 1), pltpu.roll(before, 8, 1))
    for target, corner, low, row in (
        (to_odd, first, 0, lambda j: j),
        (to_even, last, DEPTH, lambda j: ROWS - 1 - j),
    ):
        for j in range(DEPTH):
            target[j * PROBES : (j + 1) * PROBES, :] = own[row(j), 0:PROBES, :]
        for j in range(DEPTH - 2):
            target[SEND_PROBES + j * PROBES : SEND_PROBES + (j + 1) * PROBES, :] = own[row(j), PROBES : 2 * PROBES, :]
        for f in range(3):
            target[SEND_FIELDS + f * DEPTH : SEND_FIELDS + (f + 1) * DEPTH, :] = fields[f, low : low + DEPTH, :]
        target[SEND_CORNER:, :] = corner


TALL = ROWS + 2 * DEPTH
INSIDE = dict(mp=(8, 24), up=(9, 23), mw=(8, 24), i0=(9, 23), p0=(10, 22), m0=(10, 22), i1=(11, 21), p1=(12, 20), m1=(12, 20), i2=(13, 19), p2=(14, 18), m2=(14, 18), i3=(15, 17), p3=(16, 16))
NEEDED = dict(mp=(7, 25), up=(8, 24), mw=(0, 32), i0=(1, 31), p0=(2, 30), m0=(2, 30), i1=(3, 29), p1=(4, 28), m1=(4, 28), i2=(5, 27), p2=(6, 26), m2=(6, 26), i3=(7, 25), p3=(8, 24))
HELD = tuple(name for name in INSIDE if name != "p3")
HALF = ROWS // 2


def fill_coef(coef, at, wet, diag, scaled):
    coef[at, 0:1, :] = wet
    coef[at, 1:2, :] = diag
    coef[at, 2:3, :] = wet * scaled
    coef[at, 3:4, :] = GAIN * wet
    coef[at, 4:5, :] = GAIN * ((1.0 - wet) - SHIFT)


def march(rows, coef, warm, probe, get, put):
    def stencil(name, r):
        here = get(name, r)
        around = get(name, r - 1) + get(name, r + 1)
        around = around + (pltpu.roll(here, 1, 1) + pltpu.roll(here, 2 * LANES - 1, 1))
        return coef(r, 1) * here - around

    for r in rows("mp"):
        put("mp", r, coef(r, 0) * probe(r))
    for r in rows("mw"):
        put("mw", r, coef(r, 0) * warm(r))
    for r in rows("i0"):
        put("i0", r, coef(r, 2) * stencil("mw", r))
    for r in rows("up"):
        put("up", r, coef(r, 2) * stencil("mp", r))
    for k in range(4):
        power = f"p{k}"
        for r in rows(power):
            if k == 0:
                value = probe(r) - (coef(r, 0) * stencil("i0", r) + (1.0 - coef(r, 0)) * warm(r))
            else:
                value = coef(r, 3) * stencil(f"i{k}", r) + coef(r, 4) * get(f"p{k - 1}", r)
            put(power, r, value)
            if k < 3:
                put(f"m{k}", r, coef(r, 0) * value)
        for r in rows(f"i{k + 1}"):
            put(f"i{k + 1}", r, coef(r, 2) * stencil(f"m{k}", r))


def inside_kernel(axes, own, from_odd, from_even, wide, coefs, *held):
    odd_lat, _ = parities(axes)
    held = dict(zip(HELD, held, strict=True))
    lane = lax.broadcasted_iota(jnp.int32, (FIELDS, LANES), 1)
    before, after = sides(odd_lat, from_even[...], from_odd[...])
    for i in range(ROWS):
        turn = (LANES - 8 * i) % LANES
        wide[i, :, 0:LANES] = own[i]
        wide[i, :, LANES:] = jnp.where(lane < 64, pltpu.roll(after, turn, 1), pltpu.roll(before, turn, 1))
        fill_coef(coefs, i, wide[i, 64:65, :], wide[i, 65:66, :], wide[i, 66:67, :])

    def put(name, r, value):
        held[name][r - DEPTH] = value

    march(
        lambda name: range(*INSIDE.get(name, (0, 0))),
        lambda r, n: coefs[r - DEPTH, n : n + 1, :],
        lambda r: wide[r - DEPTH, 0:PROBES, :],
        lambda r: wide[r - DEPTH, PROBES : 2 * PROBES, :],
        lambda name, r: held[name][r - DEPTH],
        put,
    )


def half_kernel(behind, own_wide, own_coefs, *refs):
    held = dict(zip(HELD, refs, strict=False))
    refs = refs[len(HELD) :]
    if behind:
        other, message, sums, basis, images, probe_image, wide, coefs, *fresh = refs
    else:
        message, sums, basis, images, probe_image, wide, coefs, *fresh = refs
    fresh = dict(zip(NEEDED, fresh, strict=True))
    lane = lax.broadcasted_iota(jnp.int32, (FIELDS, LANES), 1)
    pair = message[SEND_CORNER:, :]
    for j in range(DEPTH):
        place = DEPTH - 1 - j if behind else j
        wide[j, 0:PROBES, 0:LANES] = message[j * PROBES : (j + 1) * PROBES, :]
        if j < DEPTH - 2:
            at = SEND_PROBES + j * PROBES
            wide[j, PROBES : 2 * PROBES, 0:LANES] = message[at : at + PROBES, :]
        for f in range(3):
            at = SEND_FIELDS + f * DEPTH + place
            wide[j, 2 * PROBES + f : 2 * PROBES + f + 1, 0:LANES] = message[at : at + 1, :]
        after = pltpu.roll(pair, (LANES - 8 * place) % LANES, 1)
        before = pltpu.roll(pair, (56 - 8 * place) % LANES, 1)
        wide[j, :, LANES:] = jnp.where(lane < 64, after, before)
        fill_coef(coefs, j, wide[j, 64:65, :], wide[j, 65:66, :], wide[j, 66:67, :])

    base = TALL // 2 if behind else 0

    def own(r):
        return DEPTH <= r < DEPTH + ROWS

    def halo(r):
        return r - (DEPTH + ROWS) if behind else DEPTH - 1 - r

    def rows(name):
        if name not in NEEDED:
            return range(0)
        return range(INSIDE[name][1], NEEDED[name][1]) if behind else range(NEEDED[name][0], INSIDE[name][0])

    def get(name, r):
        return fresh[name][r - base] if r in rows(name) else held[name][r - DEPTH]

    def put(name, r, value):
        fresh[name][r - base] = value

    def coef(r, n):
        return own_coefs[r - DEPTH, n : n + 1, :] if own(r) else coefs[halo(r), n : n + 1, :]

    def argument(r, at):
        return own_wide[r - DEPTH, at : at + PROBES, :] if own(r) else wide[halo(r), at : at + PROBES, :]

    march(rows, coef, lambda r: argument(r, 0), lambda r: argument(r, PROBES), get, put)

    total = other[...] if behind else jnp.zeros((3 * PROBES, 4 * PROBES), jnp.float32)
    for i in range(HALF):
        r = DEPTH + i + (HALF if behind else 0)
        for k in range(4):
            at = slice(k * PROBES, (k + 1) * PROBES)
            basis[i, at, :] = get(f"p{k}", r)[:, 0:LANES]
            images[i, at, :] = get(f"i{(k + 1) % 4}", r)[:, 0:LANES]
        probe_image[i] = get("up", r)[:, 0:LANES]
        if i % 2 == 0:
            continue
        block = jnp.concatenate([basis[i - 1], basis[i]], axis=1)
        total = total + lax.dot_general(
            block[0 : 3 * PROBES],
            block,
            (((1,), (1,)), ((), ())),
            precision=lax.Precision.HIGHEST,
            preferred_element_type=jnp.float32,
        )
    if not behind:
        sums[...] = total
        return
    lane = lax.broadcasted_iota(jnp.int32, (PROBES, LANES), 1)
    row = lax.broadcasted_iota(jnp.int32, (PROBES, LANES), 0)
    packed = jnp.zeros((PROBES, LANES), jnp.float32)
    for b in range(3):
        even = total[b * PROBES : (b + 1) * PROBES]
        odd = pltpu.roll(even, LANES - PROBES, 1)
        column = lane - b * PROBES
        inside = (column >= 0) & (column < PROBES)
        packed = jnp.where(inside, jnp.where(column >= row, even, odd), packed)
        odd_diagonal = jnp.sum(jnp.where(column == row, odd, 0.0), axis=1, keepdims=True)
        packed = jnp.where(lane == 3 * PROBES + b, odd_diagonal, packed)
    sums[...] = packed


def dot(left, right, precision):
    return jnp.dot(left, right, precision=precision, preferred_element_type=jnp.float32)


def invert_pair(p):
    scale = 1.0 / (p[0][0] * p[1][1] - p[0][1] * p[0][1])
    return p[1][1] * scale, -p[0][1] * scale, p[0][0] * scale


def prepare(p):
    n = len(p)
    if n == 2:
        a, b, c = invert_pair(p)
        return lambda r: [a * r[0] + b * r[1], b * r[0] + c * r[1]]
    h = n // 2
    top = prepare([row[:h] for row in p[:h]])
    side = [row[h:] for row in p[:h]]
    solved = list(zip(*[top([side[i][j] for i in range(h)]) for j in range(h)], strict=True))

    def product(rows, weights):
        terms = [row * weight for row, weight in zip(rows, weights, strict=True)]
        while len(terms) > 1:
            terms = [sum(terms[i : i + 2][1:], terms[i]) for i in range(0, len(terms), 2)]
        return terms[0]

    rest = [[None] * h for _ in range(h)]
    for i in range(h):
        for j in range(i, h):
            rest[i][j] = p[h + i][h + j] - product([side[t][i] for t in range(h)], [solved[t][j] for t in range(h)])
            rest[j][i] = rest[i][j]
    bottom = prepare(rest)

    def solve(r):
        upper = top(r[:h])
        lower = bottom([r[h + i] - product([side[t][i] for t in range(h)], upper) for i in range(h)])
        return [upper[t] - product(solved[t], lower) for t in range(h)] + lower

    return solve


def eliminate(parts):
    row = lax.broadcasted_iota(jnp.int32, (8, LANES), 0)

    def spread(value):
        return jnp.broadcast_to(value, (8, LANES))

    def take(part, lane):
        return jnp.take_along_axis(part, jnp.full((8, LANES), lane, jnp.int32), axis=1)

    for home in range(len(parts)):
        at = 8 * home
        column = [take(parts[home], at + j) for j in range(8)]
        pivot = [[spread(column[j][i : i + 1]) for j in range(8)] for i in range(8)]
        solved = prepare(pivot)([spread(parts[home][i : i + 1]) for i in range(8)])
        for v in [*range(home, len(parts)), *range(home)]:
            if v == home:
                part = solved[0]
                for i in range(1, 8):
                    part = jnp.where(row == i, solved[i], part)
                parts[v] = part
            else:
                terms = [take(parts[v], at + j) * solved[j] for j in range(8)]
                parts[v] = parts[v] - (
                    ((terms[0] + terms[1]) + (terms[2] + terms[3])) + ((terms[4] + terms[5]) + (terms[6] + terms[7]))
                )
    return parts


def finish_kernel(
    axes,
    sums, own, basis_first, basis_last, images_first, images_last, probe_first, probe_last,
    solution_out, residual_out, grad_out,
    coeffs, rows,
):
    _, odd_lon = parities(axes)
    packed = sums[...]
    flipped = packed.T
    lane = lax.broadcasted_iota(jnp.int32, (PROBES, PROBES), 1)
    row = lax.broadcasted_iota(jnp.int32, (PROBES, PROBES), 0)
    moments = []
    for b in range(3):
        block = packed[:, b * PROBES : (b + 1) * PROBES]
        mirror = flipped[b * PROBES : (b + 1) * PROBES, :]
        moments.append(jnp.where(lane >= row, block, mirror))
        odd = jnp.where(lane < row, block, mirror)
        moments.append(jnp.where(lane == row, packed[:, 3 * PROBES + b : 3 * PROBES + b + 1], odd))
    power = [moments[k + 1] * (1.0 / GAIN) + moments[k] * SHIFT for k in range(5)]

    table = jnp.concatenate(
        [jnp.concatenate([power[b], power[b + 1], power[b + 2], moments[b]], axis=1) for b in range(3)], axis=0
    )
    parts = eliminate([table[8 * v : 8 * v + 8] for v in range(12)])
    solved = jnp.concatenate(parts, axis=0)

    t = [jnp.sum(jnp.where(lane == row, m, 0.0), axis=(0, 1), keepdims=True) for m in moments]
    a = t[1] / t[0]
    n1 = t[2] - a * t[1]
    b0, b1 = (t[2] / t[0], (t[3] - a * t[2]) / n1)
    b2 = b1 * a - b0
    c0, c1 = (t[3] / t[0], (t[4] - a * t[3]) / n1)
    c2 = (t[5] - b1 * t[4] + b2 * t[3]) / (t[4] - b1 * t[3] + b2 * t[2])

    nothing = jnp.zeros((PROBES, LANES), jnp.float32)
    wide_lane = lax.broadcasted_iota(jnp.int32, (4 * PROBES, LANES), 1)
    wide_row = lax.broadcasted_iota(jnp.int32, (4 * PROBES, LANES), 0)
    one = (wide_lane == wide_row + 3 * PROBES).astype(jnp.float32)
    kept = jnp.concatenate([solved, nothing], axis=0)
    left = one - SHIFT * kept - (1.0 / GAIN) * jnp.concatenate([nothing, solved], axis=0)

    def for_polynomials(v):
        v = [v[k * PROBES : (k + 1) * PROBES] for k in range(4)]
        return jnp.concatenate(
            [v[0] + a * v[1] + b0 * v[2] + c0 * v[3], v[1] + b1 * v[2] + c1 * v[3], v[2] + c2 * v[3], v[3]], axis=0
        )

    columns = jnp.where(
        wide_lane < PROBES,
        pltpu.roll(for_polynomials(kept), PROBES, 1),
        jnp.where(wide_lane < 2 * PROBES, pltpu.roll(for_polynomials(left), 2 * PROBES, 1), pltpu.roll(kept, 3 * PROBES, 1)),
    )
    coeffs[...] = columns.T[0 : 3 * PROBES]
    weights = coeffs[2 * PROBES :, :] + one[0:PROBES]
    a, b0, b1, c0, c1, c2 = (jnp.broadcast_to(x, (PROBES, LANES)) for x in (a, b0, b1, c0, c1, c2))

    for i in range(0, ROWS, 2):
        j = i % HALF
        basis, images, probe_image = (
            (basis_first, images_first, probe_first) if i < HALF else (basis_last, images_last, probe_last)
        )
        polynomials = []
        for n in (j, j + 1):
            v0 = basis[n, 0:PROBES, :]
            w1 = basis[n, PROBES : 2 * PROBES, :] - a * v0
            w2 = basis[n, 2 * PROBES : 3 * PROBES, :] - b1 * w1 - b0 * v0
            w3 = basis[n, 3 * PROBES :, :] - c2 * w2 - c1 * w1 - c0 * v0
            polynomials.append(jnp.concatenate([v0, w1, w2, w3], axis=0))
        both = dot(coeffs[0 : 2 * PROBES, :], jnp.concatenate(polynomials, axis=1), lax.Precision.HIGH)
        image = dot(weights, jnp.concatenate([images[j], images[j + 1]], axis=1), lax.Precision.HIGH)
        for n in range(2):
            lanes = slice(n * LANES, (n + 1) * LANES)
            values = both[0:PROBES, lanes] + own[i + n, 0:PROBES, :]
            terms = values * probe_image[j + n] + image[:, lanes] * own[i + n, PROBES : 2 * PROBES, :]
            wet = own[i + n, 64:65, :]
            out = rows.at[jnp.where(odd_lon == 0, i + n, ROWS - 1 - i - n)]
            out[0:PROBES, :] = values
            out[PROBES : 2 * PROBES, :] = both[PROBES:, lanes]
            out[2 * PROBES : 2 * PROBES + 1, :] = wet * (jnp.sum(terms, axis=0, keepdims=True) * (1.0 / PROBES))
    for p in range(ROWS):
        solution_out[:, p, :] = rows[p, 0:PROBES, :]
        residual_out[:, p, :] = rows[p, PROBES : 2 * PROBES, :]
        grad_out[p : p + 1, :] = rows[p, 2 * PROBES : 2 * PROBES + 1, :]


def f32(*shape):
    return jax.ShapeDtypeStruct(shape, jnp.float32)


def exchanged(value, axes, odd, wrap):
    size = lax.axis_size(axes)
    pairs = []
    for i in range(size):
        other = ((i + odd) ^ 1) - odd
        if wrap or 0 <= other < size:
            pairs.append((i, other % size))
    return lax.ppermute(value, axes, pairs)


def spread_sum(value, axes):
    size = lax.axis_size(axes)
    copies = jnp.broadcast_to(value[None], (size,) + value.shape)
    return jnp.sum(lax.all_to_all(copies, axes, 0, 0), axis=0)


def make_local(lat, lon, stages):
    axes = (lat[-1], lon[-1])

    def local(warm_start, probe_signs, ocean_mask, kappa_sq, scale_field):
        args = (warm_start, probe_signs, ocean_mask, kappa_sq, scale_field)
        own, fields, to_odd, to_even = pl.pallas_call(
            functools.partial(pack_kernel, axes),
            out_shape=(
                f32(ROWS, FIELDS, LANES),
                f32(3, ROWS, LANES),
                f32(FIELDS, LANES),
                f32(FIELDS, LANES),
            ),
            in_specs=[pl.BlockSpec(memory_space=pltpu.HBM)] * 5,
            scratch_shapes=[pltpu.VMEM(x.shape, x.dtype) for x in args] + [pltpu.SemaphoreType.DMA((5,))],
            compiler_params=PARAMS,
            name="pack_edges",
        )(*(pltpu.with_memory_space_constraint(x, pltpu.HBM) for x in args))
        odd_lat = exchanged(to_odd, lat, 1, False)
        even_lat = exchanged(to_even, lat, 0, False)
        to_odd, to_even = pl.pallas_call(
            functools.partial(send_kernel, axes),
            out_shape=(f32(SEND_ROWS, LANES), f32(SEND_ROWS, LANES)),
            compiler_params=PARAMS,
            name="pack_rows",
        )(own, fields, odd_lat, even_lat)
        odd_lon = exchanged(to_odd, lon, 1, True)
        even_lon = exchanged(to_even, lon, 0, True)
        inside = pl.pallas_call(
            functools.partial(inside_kernel, axes),
            out_shape=(f32(ROWS, FIELDS, 2 * LANES), f32(ROWS, 8, 2 * LANES))
            + (f32(ROWS, PROBES, 2 * LANES),) * len(HELD),
            compiler_params=PARAMS,
            cost_estimate=pl.CostEstimate(flops=40_000_000, bytes_accessed=8_000_000, transcendentals=0),
            name="inside_rows",
        )(own, odd_lat, even_lat)
        half = dict(
            scratch_shapes=[
                pltpu.VMEM((DEPTH, FIELDS, 2 * LANES), jnp.float32),
                pltpu.VMEM((DEPTH, 8, 2 * LANES), jnp.float32),
            ]
            + [pltpu.VMEM((TALL // 2, PROBES, 2 * LANES), jnp.float32)] * len(NEEDED),
            compiler_params=PARAMS,
            cost_estimate=pl.CostEstimate(flops=40_000_000, bytes_accessed=8_000_000, transcendentals=0),
        )
        filled = (f32(HALF, 4 * PROBES, LANES), f32(HALF, 4 * PROBES, LANES), f32(HALF, PROBES, LANES))
        part, *first = pl.pallas_call(
            functools.partial(half_kernel, False),
            out_shape=(f32(3 * PROBES, LANES), *filled),
            name="first_rows",
            **half,
        )(*inside, odd_lon)
        sums, *last = pl.pallas_call(
            functools.partial(half_kernel, True),
            out_shape=(f32(PROBES, LANES), *filled),
            name="last_rows",
            **half,
        )(*inside, part, even_lon)
        with jax.named_scope("sum_moments"):
            for group in stages:
                sums = spread_sum(sums, group)
        return pl.pallas_call(
            functools.partial(finish_kernel, axes),
            out_shape=(
                f32(PROBES, ROWS, LANES),
                f32(PROBES, ROWS, LANES),
                f32(ROWS, LANES),
            ),
            scratch_shapes=[
                pltpu.VMEM((3 * PROBES, 4 * PROBES), jnp.float32),
                pltpu.VMEM((ROWS, FIELDS, LANES), jnp.float32),
            ],
            compiler_params=PARAMS,
            name="solve_and_combine",
        )(sums, own, *(x for pair in zip(first, last, strict=True) for x in pair))

    return local


def solution(mesh):
    if mesh.devices.shape == (16, 32):
        grid = Mesh(mesh.devices.reshape(2, 4, 2, 4, 8), ("zh", "x", "c", "zl", "y"))
        lat, lon = (("zh", "x", "c"), ("zl", "y"))
        stages = (("x", "c"), ("y",), ("zh", "zl"))
    else:
        grid, lat, lon, stages = (mesh, ("lat",), ("lon",), (("lat",), ("lon",)))
    return jax.shard_map(
        make_local(lat, lon, stages),
        mesh=grid,
        in_specs=(P(None, lon, lat), P(None, lon, lat), P(lon, lat), P(lon, lat), P(lon, lat)),
        out_specs=(P(None, lon, lat), P(None, lon, lat), P(lon, lat)),
        check_vma=False,
    )
```

```python
import functools

import jax
import jax.numpy as jnp
from jax import lax
from jax.experimental import pallas as pl
from jax.experimental.pallas import tpu as pltpu
from jax.sharding import Mesh
from jax.sharding import PartitionSpec as P

PROBES = 32
DEPTH = 8
ROWS = 16
LANES = 128
FIELDS = 72
SHIFT = 1.2
GAIN = 0.25
PARAMS = pltpu.CompilerParams(vmem_limit_bytes=32 * 1024 * 1024)


def parities(axes):
    return tuple(lax.rem(lax.axis_index(axis), 2) for axis in axes)


def pack_kernel(axes, warm_hbm, signs_hbm, mask_hbm, kappa_hbm, scale_hbm, own, fields, to_odd, to_even, *scratch):
    odd, odd_lon = parities(axes)
    sems = scratch[-1]
    copies = [
        pltpu.make_async_copy(source, target, sems.at[n])
        for n, (source, target) in enumerate(
            zip((warm_hbm, signs_hbm, mask_hbm, kappa_hbm, scale_hbm), scratch[:-1], strict=True)
        )
    ]
    for copy in copies:
        copy.start()
    warm, signs, mask, kappa, scale = scratch[:-1]
    rows = [own.at[jnp.where(odd_lon == 0, p, ROWS - 1 - p)] for p in range(ROWS)]
    copies[0].wait()
    for p, row in enumerate(rows):
        row[0:PROBES, :] = warm[:, p, :]
    copies[1].wait()
    for p, row in enumerate(rows):
        row[PROBES : 2 * PROBES, :] = 2.0 * signs[:, p, :].astype(jnp.float32) - 1.0
    for copy in copies[2:]:
        copy.wait()
    wet = mask[...].astype(jnp.float32)
    diag = kappa[...] + 4.0
    scaled = scale[...]
    for p, row in enumerate(rows):
        row[2 * PROBES :, :] = jnp.concatenate(
            [wet[p : p + 1], diag[p : p + 1], scaled[p : p + 1], jnp.zeros((5, LANES), jnp.float32)], axis=0
        )
    block = lax.broadcasted_iota(jnp.int32, (FIELDS, LANES), 1) // DEPTH
    left_edge = jnp.zeros((FIELDS, LANES), jnp.float32)
    right_edge = jnp.zeros((FIELDS, LANES), jnp.float32)
    for i in range(ROWS):
        row = own[i]
        for f in range(3):
            fields[f, i : i + 1, :] = row[2 * PROBES + f : 2 * PROBES + f + 1]
        turned = pltpu.roll(row, DEPTH * i, 1) if i else row
        left_edge = jnp.where(block == i, turned, left_edge)
        right_edge = jnp.where(block == (i - 1) % ROWS, turned, right_edge)
    to_even[...] = jnp.where(odd == 0, right_edge, left_edge)
    to_odd[...] = jnp.where(odd == 0, left_edge, right_edge)


def sides(odd, even_side, odd_side):
    return jnp.where(odd == 0, odd_side, even_side), jnp.where(odd == 0, even_side, odd_side)


SEND_PROBES = DEPTH * PROBES
SEND_FIELDS = SEND_PROBES + (DEPTH - 2) * PROBES
SEND_CORNER = SEND_FIELDS + 3 * DEPTH
SEND_ROWS = SEND_CORNER + FIELDS


def send_kernel(axes, own, fields, from_odd, from_even, to_odd, to_even):
    odd_lat, _ = parities(axes)
    lane = lax.broadcasted_iota(jnp.int32, (FIELDS, LANES), 1)
    before, after = sides(odd_lat, from_even[...], from_odd[...])
    first = jnp.where(lane < 64, after, pltpu.roll(before, 72, 1))
    last = jnp.where(lane < 64, pltpu.roll(after, 64, 1), pltpu.roll(before, 8, 1))
    for target, corner, low, row in (
        (to_odd, first, 0, lambda j: j),
        (to_even, last, DEPTH, lambda j: ROWS - 1 - j),
    ):
        for j in range(DEPTH):
            target[j * PROBES : (j + 1) * PROBES, :] = own[row(j), 0:PROBES, :]
        for j in range(DEPTH - 2):
            target[SEND_PROBES + j * PROBES : SEND_PROBES + (j + 1) * PROBES, :] = own[row(j), PROBES : 2 * PROBES, :]
        for f in range(3):
            target[SEND_FIELDS + f * DEPTH : SEND_FIELDS + (f + 1) * DEPTH, :] = fields[f, low : low + DEPTH, :]
        target[SEND_CORNER:, :] = corner


TALL = ROWS + 2 * DEPTH
INSIDE = dict(mp=(8, 24), up=(9, 23), mw=(8, 24), i0=(9, 23), p0=(10, 22), m0=(10, 22), i1=(11, 21), p1=(12, 20), m1=(12, 20), i2=(13, 19), p2=(14, 18), m2=(14, 18), i3=(15, 17), p3=(16, 16))
NEEDED = dict(mp=(7, 25), up=(8, 24), mw=(0, 32), i0=(1, 31), p0=(2, 30), m0=(2, 30), i1=(3, 29), p1=(4, 28), m1=(4, 28), i2=(5, 27), p2=(6, 26), m2=(6, 26), i3=(7, 25), p3=(8, 24))
HELD = tuple(name for name in INSIDE if name != "p3")
HALF = ROWS // 2


def fill_coef(coef, at, wet, diag, scaled):
    coef[at, 0:1, :] = wet
    coef[at, 1:2, :] = diag
    coef[at, 2:3, :] = wet * scaled
    coef[at, 3:4, :] = GAIN * wet
    coef[at, 4:5, :] = GAIN * ((1.0 - wet) - SHIFT)


def march(rows, coef, warm, probe, get, put):
    def stencil(name, r):
        here = get(name, r)
        around = get(name, r - 1) + get(name, r + 1)
        around = around + (pltpu.roll(here, 1, 1) + pltpu.roll(here, 2 * LANES - 1, 1))
        return coef(r, 1) * here - around

    for r in rows("mp"):
        put("mp", r, coef(r, 0) * probe(r))
    for r in rows("mw"):
        put("mw", r, coef(r, 0) * warm(r))
    for r in rows("i0"):
        put("i0", r, coef(r, 2) * stencil("mw", r))
    for r in rows("up"):
        put("up", r, coef(r, 2) * stencil("mp", r))
    for k in range(4):
        power = f"p{k}"
        for r in rows(power):
            if k == 0:
                value = probe(r) - (coef(r, 0) * stencil("i0", r) + (1.0 - coef(r, 0)) * warm(r))
            else:
                value = coef(r, 3) * stencil(f"i{k}", r) + coef(r, 4) * get(f"p{k - 1}", r)
            put(power, r, value)
            if k < 3:
                put(f"m{k}", r, coef(r, 0) * value)
        for r in rows(f"i{k + 1}"):
            put(f"i{k + 1}", r, coef(r, 2) * stencil(f"m{k}", r))


def inside_kernel(axes, own, from_odd, from_even, wide, coefs, *held):
    odd_lat, _ = parities(axes)
    held = dict(zip(HELD, held, strict=True))
    lane = lax.broadcasted_iota(jnp.int32, (FIELDS, LANES), 1)
    before, after = sides(odd_lat, from_even[...], from_odd[...])
    for i in range(ROWS):
        turn = (LANES - 8 * i) % LANES
        wide[i, :, 0:LANES] = own[i]
        wide[i, :, LANES:] = jnp.where(lane < 64, pltpu.roll(after, turn, 1), pltpu.roll(before, turn, 1))
        fill_coef(coefs, i, wide[i, 64:65, :], wide[i, 65:66, :], wide[i, 66:67, :])

    def put(name, r, value):
        held[name][r - DEPTH] = value

    march(
        lambda name: range(*INSIDE.get(name, (0, 0))),
        lambda r, n: coefs[r - DEPTH, n : n + 1, :],
        lambda r: wide[r - DEPTH, 0:PROBES, :],
        lambda r: wide[r - DEPTH, PROBES : 2 * PROBES, :],
        lambda name, r: held[name][r - DEPTH],
        put,
    )


def half_kernel(behind, own_wide, own_coefs, *refs):
    held = dict(zip(HELD, refs, strict=False))
    refs = refs[len(HELD) :]
    if behind:
        other, message, sums, basis, images, probe_image, wide, coefs, *fresh = refs
    else:
        message, sums, basis, images, probe_image, wide, coefs, *fresh = refs
    fresh = dict(zip(NEEDED, fresh, strict=True))
    lane = lax.broadcasted_iota(jnp.int32, (FIELDS, LANES), 1)
    pair = message[SEND_CORNER:, :]
    for j in range(DEPTH):
        place = DEPTH - 1 - j if behind else j
        wide[j, 0:PROBES, 0:LANES] = message[j * PROBES : (j + 1) * PROBES, :]
        if j < DEPTH - 2:
            at = SEND_PROBES + j * PROBES
            wide[j, PROBES : 2 * PROBES, 0:LANES] = message[at : at + PROBES, :]
        for f in range(3):
            at = SEND_FIELDS + f * DEPTH + place
            wide[j, 2 * PROBES + f : 2 * PROBES + f + 1, 0:LANES] = message[at : at + 1, :]
        after = pltpu.roll(pair, (LANES - 8 * place) % LANES, 1)
        before = pltpu.roll(pair, (56 - 8 * place) % LANES, 1)
        wide[j, :, LANES:] = jnp.where(lane < 64, after, before)
        fill_coef(coefs, j, wide[j, 64:65, :], wide[j, 65:66, :], wide[j, 66:67, :])

    base = TALL // 2 if behind else 0

    def own(r):
        return DEPTH <= r < DEPTH + ROWS

    def halo(r):
        return r - (DEPTH + ROWS) if behind else DEPTH - 1 - r

    def rows(name):
        if name not in NEEDED:
            return range(0)
        return range(INSIDE[name][1], NEEDED[name][1]) if behind else range(NEEDED[name][0], INSIDE[name][0])

    def get(name, r, lanes=2 * LANES):
        return fresh[name][r - base, :, 0:lanes] if r in rows(name) else held[name][r - DEPTH, :, 0:lanes]

    def put(name, r, value):
        if name in ("p3", "up"):
            fresh[name][r - base, :, 0:LANES] = value[:, 0:LANES]
        else:
            fresh[name][r - base] = value

    def coef(r, n):
        return own_coefs[r - DEPTH, n : n + 1, :] if own(r) else coefs[halo(r), n : n + 1, :]

    def argument(r, at):
        return own_wide[r - DEPTH, at : at + PROBES, :] if own(r) else wide[halo(r), at : at + PROBES, :]

    march(rows, coef, lambda r: argument(r, 0), lambda r: argument(r, PROBES), get, put)

    total = other[...] if behind else jnp.zeros((3 * PROBES, 4 * PROBES), jnp.float32)
    for i in range(HALF):
        r = DEPTH + i + (HALF if behind else 0)
        for k in range(4):
            at = slice(k * PROBES, (k + 1) * PROBES)
            basis[i, at, :] = get(f"p{k}", r, LANES)
            images[i, at, :] = get(f"i{(k + 1) % 4}", r, LANES)
        probe_image[i] = get("up", r, LANES)
        if i % 2 == 0:
            continue
        block = jnp.concatenate([basis[i - 1], basis[i]], axis=1)
        total = total + lax.dot_general(
            block[0 : 3 * PROBES],
            block,
            (((1,), (1,)), ((), ())),
            precision=lax.Precision.HIGHEST,
            preferred_element_type=jnp.float32,
        )
    if not behind:
        sums[...] = total
        return
    lane = lax.broadcasted_iota(jnp.int32, (PROBES, LANES), 1)
    row = lax.broadcasted_iota(jnp.int32, (PROBES, LANES), 0)
    packed = jnp.zeros((PROBES, LANES), jnp.float32)
    for b in range(3):
        even = total[b * PROBES : (b + 1) * PROBES]
        odd = pltpu.roll(even, LANES - PROBES, 1)
        column = lane - b * PROBES
        inside = (column >= 0) & (column < PROBES)
        packed = jnp.where(inside, jnp.where(column >= row, even, odd), packed)
        odd_diagonal = jnp.sum(jnp.where(column == row, odd, 0.0), axis=1, keepdims=True)
        packed = jnp.where(lane == 3 * PROBES + b, odd_diagonal, packed)
    sums[...] = packed


def dot(left, right, precision):
    return jnp.dot(left, right, precision=precision, preferred_element_type=jnp.float32)


def invert_pair(p):
    scale = 1.0 / (p[0][0] * p[1][1] - p[0][1] * p[0][1])
    return p[1][1] * scale, -p[0][1] * scale, p[0][0] * scale


def prepare(p):
    n = len(p)
    if n == 2:
        a, b, c = invert_pair(p)
        return lambda r: [a * r[0] + b * r[1], b * r[0] + c * r[1]]
    h = n // 2
    top = prepare([row[:h] for row in p[:h]])
    side = [row[h:] for row in p[:h]]
    solved = list(zip(*[top([side[i][j] for i in range(h)]) for j in range(h)], strict=True))

    def product(rows, weights):
        terms = [row * weight for row, weight in zip(rows, weights, strict=True)]
        while len(terms) > 1:
            terms = [sum(terms[i : i + 2][1:], terms[i]) for i in range(0, len(terms), 2)]
        return terms[0]

    rest = [[None] * h for _ in range(h)]
    for i in range(h):
        for j in range(i, h):
            rest[i][j] = p[h + i][h + j] - product([side[t][i] for t in range(h)], [solved[t][j] for t in range(h)])
            rest[j][i] = rest[i][j]
    bottom = prepare(rest)

    def solve(r):
        upper = top(r[:h])
        lower = bottom([r[h + i] - product([side[t][i] for t in range(h)], upper) for i in range(h)])
        return [upper[t] - product(solved[t], lower) for t in range(h)] + lower

    return solve


def eliminate(parts):
    row = lax.broadcasted_iota(jnp.int32, (8, LANES), 0)

    def spread(value):
        return jnp.broadcast_to(value, (8, LANES))

    def take(part, lane):
        return jnp.take_along_axis(part, jnp.full((8, LANES), lane, jnp.int32), axis=1)

    for home in range(len(parts)):
        at = 8 * home
        column = [take(parts[home], at + j) for j in range(8)]
        pivot = [[spread(column[j][i : i + 1]) for j in range(8)] for i in range(8)]
        solved = prepare(pivot)([spread(parts[home][i : i + 1]) for i in range(8)])
        for v in [*range(home, len(parts)), *range(home)]:
            if v == home:
                part = solved[0]
                for i in range(1, 8):
                    part = jnp.where(row == i, solved[i], part)
                parts[v] = part
            else:
                terms = [take(parts[v], at + j) * solved[j] for j in range(8)]
                parts[v] = parts[v] - (
                    ((terms[0] + terms[1]) + (terms[2] + terms[3])) + ((terms[4] + terms[5]) + (terms[6] + terms[7]))
                )
    return parts


def finish_kernel(
    axes,
    sums, own, basis_first, basis_last, images_first, images_last, probe_first, probe_last,
    solution_out, residual_out, grad_out,
    coeffs, rows,
):
    _, odd_lon = parities(axes)
    packed = sums[...]
    flipped = packed.T
    lane = lax.broadcasted_iota(jnp.int32, (PROBES, PROBES), 1)
    row = lax.broadcasted_iota(jnp.int32, (PROBES, PROBES), 0)
    moments = []
    for b in range(3):
        block = packed[:, b * PROBES : (b + 1) * PROBES]
        mirror = flipped[b * PROBES : (b + 1) * PROBES, :]
        moments.append(jnp.where(lane >= row, block, mirror))
        odd = jnp.where(lane < row, block, mirror)
        moments.append(jnp.where(lane == row, packed[:, 3 * PROBES + b : 3 * PROBES + b + 1], odd))
    power = [moments[k + 1] * (1.0 / GAIN) + moments[k] * SHIFT for k in range(5)]

    table = jnp.concatenate(
        [jnp.concatenate([power[b], power[b + 1], power[b + 2], moments[b]], axis=1) for b in range(3)], axis=0
    )
    parts = eliminate([table[8 * v : 8 * v + 8] for v in range(12)])
    solved = jnp.concatenate(parts, axis=0)

    t = [jnp.sum(jnp.where(lane == row, m, 0.0), axis=(0, 1), keepdims=True) for m in moments]
    a = t[1] / t[0]
    n1 = t[2] - a * t[1]
    b0, b1 = (t[2] / t[0], (t[3] - a * t[2]) / n1)
    b2 = b1 * a - b0
    c0, c1 = (t[3] / t[0], (t[4] - a * t[3]) / n1)
    c2 = (t[5] - b1 * t[4] + b2 * t[3]) / (t[4] - b1 * t[3] + b2 * t[2])

    nothing = jnp.zeros((PROBES, LANES), jnp.float32)
    wide_lane = lax.broadcasted_iota(jnp.int32, (4 * PROBES, LANES), 1)
    wide_row = lax.broadcasted_iota(jnp.int32, (4 * PROBES, LANES), 0)
    one = (wide_lane == wide_row + 3 * PROBES).astype(jnp.float32)
    kept = jnp.concatenate([solved, nothing], axis=0)
    left = one - SHIFT * kept - (1.0 / GAIN) * jnp.concatenate([nothing, solved], axis=0)

    def for_polynomials(v):
        v = [v[k * PROBES : (k + 1) * PROBES] for k in range(4)]
        return jnp.concatenate(
            [v[0] + a * v[1] + b0 * v[2] + c0 * v[3], v[1] + b1 * v[2] + c1 * v[3], v[2] + c2 * v[3], v[3]], axis=0
        )

    columns = jnp.where(
        wide_lane < PROBES,
        pltpu.roll(for_polynomials(kept), PROBES, 1),
        jnp.where(wide_lane < 2 * PROBES, pltpu.roll(for_polynomials(left), 2 * PROBES, 1), pltpu.roll(kept, 3 * PROBES, 1)),
    )
    coeffs[...] = columns.T[0 : 3 * PROBES]
    weights = coeffs[2 * PROBES :, :] + one[0:PROBES]
    a, b0, b1, c0, c1, c2 = (jnp.broadcast_to(x, (PROBES, LANES)) for x in (a, b0, b1, c0, c1, c2))

    for i in range(0, ROWS, 2):
        j = i % HALF
        basis, images, probe_image = (
            (basis_first, images_first, probe_first) if i < HALF else (basis_last, images_last, probe_last)
        )
        polynomials = []
        for n in (j, j + 1):
            v0 = basis[n, 0:PROBES, :]
            w1 = basis[n, PROBES : 2 * PROBES, :] - a * v0
            w2 = basis[n, 2 * PROBES : 3 * PROBES, :] - b1 * w1 - b0 * v0
            w3 = basis[n, 3 * PROBES :, :] - c2 * w2 - c1 * w1 - c0 * v0
            polynomials.append(jnp.concatenate([v0, w1, w2, w3], axis=0))
        both = dot(coeffs[0 : 2 * PROBES, :], jnp.concatenate(polynomials, axis=1), lax.Precision.HIGH)
        image = dot(weights, jnp.concatenate([images[j], images[j + 1]], axis=1), lax.Precision.HIGH)
        for n in range(2):
            lanes = slice(n * LANES, (n + 1) * LANES)
            values = both[0:PROBES, lanes] + own[i + n, 0:PROBES, :]
            terms = values * probe_image[j + n] + image[:, lanes] * own[i + n, PROBES : 2 * PROBES, :]
            wet = own[i + n, 64:65, :]
            out = rows.at[jnp.where(odd_lon == 0, i + n, ROWS - 1 - i - n)]
            out[0:PROBES, :] = values
            out[PROBES : 2 * PROBES, :] = both[PROBES:, lanes]
            out[2 * PROBES : 2 * PROBES + 1, :] = wet * (jnp.sum(terms, axis=0, keepdims=True) * (1.0 / PROBES))
    for p in range(ROWS):
        solution_out[:, p, :] = rows[p, 0:PROBES, :]
        residual_out[:, p, :] = rows[p, PROBES : 2 * PROBES, :]
        grad_out[p : p + 1, :] = rows[p, 2 * PROBES : 2 * PROBES + 1, :]


def f32(*shape):
    return jax.ShapeDtypeStruct(shape, jnp.float32)


def exchanged(value, axes, odd, wrap):
    size = lax.axis_size(axes)
    pairs = []
    for i in range(size):
        other = ((i + odd) ^ 1) - odd
        if wrap or 0 <= other < size:
            pairs.append((i, other % size))
    return lax.ppermute(value, axes, pairs)


def spread_sum(value, axes):
    size = lax.axis_size(axes)
    copies = jnp.broadcast_to(value[None], (size,) + value.shape)
    return jnp.sum(lax.all_to_all(copies, axes, 0, 0), axis=0)


def make_local(lat, lon, stages):
    axes = (lat[-1], lon[-1])

    def local(warm_start, probe_signs, ocean_mask, kappa_sq, scale_field):
        args = (warm_start, probe_signs, ocean_mask, kappa_sq, scale_field)
        own, fields, to_odd, to_even = pl.pallas_call(
            functools.partial(pack_kernel, axes),
            out_shape=(
                f32(ROWS, FIELDS, LANES),
                f32(3, ROWS, LANES),
                f32(FIELDS, LANES),
                f32(FIELDS, LANES),
            ),
            in_specs=[pl.BlockSpec(memory_space=pltpu.HBM)] * 5,
            scratch_shapes=[pltpu.VMEM(x.shape, x.dtype) for x in args] + [pltpu.SemaphoreType.DMA((5,))],
            compiler_params=PARAMS,
            name="pack_edges",
        )(*(pltpu.with_memory_space_constraint(x, pltpu.HBM) for x in args))
        odd_lat = exchanged(to_odd, lat, 1, False)
        even_lat = exchanged(to_even, lat, 0, False)
        to_odd, to_even = pl.pallas_call(
            functools.partial(send_kernel, axes),
            out_shape=(f32(SEND_ROWS, LANES), f32(SEND_ROWS, LANES)),
            compiler_params=PARAMS,
            name="pack_rows",
        )(own, fields, odd_lat, even_lat)
        odd_lon = exchanged(to_odd, lon, 1, True)
        even_lon = exchanged(to_even, lon, 0, True)
        inside = pl.pallas_call(
            functools.partial(inside_kernel, axes),
            out_shape=(f32(ROWS, FIELDS, 2 * LANES), f32(ROWS, 8, 2 * LANES))
            + (f32(ROWS, PROBES, 2 * LANES),) * len(HELD),
            compiler_params=PARAMS,
            cost_estimate=pl.CostEstimate(flops=40_000_000, bytes_accessed=8_000_000, transcendentals=0),
            name="inside_rows",
        )(own, odd_lat, even_lat)
        half = dict(
            scratch_shapes=[
                pltpu.VMEM((DEPTH, FIELDS, 2 * LANES), jnp.float32),
                pltpu.VMEM((DEPTH, 8, 2 * LANES), jnp.float32),
            ]
            + [pltpu.VMEM((TALL // 2, PROBES, 2 * LANES), jnp.float32)] * len(NEEDED),
            compiler_params=PARAMS,
            cost_estimate=pl.CostEstimate(flops=40_000_000, bytes_accessed=8_000_000, transcendentals=0),
        )
        filled = (f32(HALF, 4 * PROBES, LANES), f32(HALF, 4 * PROBES, LANES), f32(HALF, PROBES, LANES))
        part, *first = pl.pallas_call(
            functools.partial(half_kernel, False),
            out_shape=(f32(3 * PROBES, LANES), *filled),
            name="first_rows",
            **half,
        )(*inside, odd_lon)
        sums, *last = pl.pallas_call(
            functools.partial(half_kernel, True),
            out_shape=(f32(PROBES, LANES), *filled),
            name="last_rows",
            **half,
        )(*inside, part, even_lon)
        with jax.named_scope("sum_moments"):
            for group in stages:
                sums = spread_sum(sums, group)
        return pl.pallas_call(
            functools.partial(finish_kernel, axes),
            out_shape=(
                f32(PROBES, ROWS, LANES),
                f32(PROBES, ROWS, LANES),
                f32(ROWS, LANES),
            ),
            scratch_shapes=[
                pltpu.VMEM((3 * PROBES, 4 * PROBES), jnp.float32),
                pltpu.VMEM((ROWS, FIELDS, LANES), jnp.float32),
            ],
            compiler_params=PARAMS,
            name="solve_and_combine",
        )(sums, own, *(x for pair in zip(first, last, strict=True) for x in pair))

    return local


def solution(mesh):
    if mesh.devices.shape == (16, 32):
        grid = Mesh(mesh.devices.reshape(2, 4, 2, 4, 8), ("zh", "x", "c", "zl", "y"))
        lat, lon = (("zh", "x", "c"), ("zl", "y"))
        stages = (("x", "c"), ("zh", "zl"), ("y",))
    else:
        grid, lat, lon, stages = (mesh, ("lat",), ("lon",), (("lat",), ("lon",)))
    return jax.shard_map(
        make_local(lat, lon, stages),
        mesh=grid,
        in_specs=(P(None, lon, lat), P(None, lon, lat), P(lon, lat), P(lon, lat), P(lon, lat)),
        out_specs=(P(None, lon, lat), P(None, lon, lat), P(lon, lat)),
        check_vma=False,
    )
```

```python
import functools

import jax
import jax.numpy as jnp
from jax import lax
from jax.experimental import pallas as pl
from jax.experimental.pallas import tpu as pltpu
from jax.sharding import Mesh
from jax.sharding import PartitionSpec as P

PROBES = 32
DEPTH = 8
ROWS = 16
LANES = 128
FIELDS = 72
SHIFT = 1.2
GAIN = 0.25
PARAMS = pltpu.CompilerParams(vmem_limit_bytes=32 * 1024 * 1024)


def parities(axes):
    return tuple(lax.rem(lax.axis_index(axis), 2) for axis in axes)


def pack_kernel(axes, warm_hbm, signs_hbm, mask_hbm, kappa_hbm, scale_hbm, own, fields, to_odd, to_even, *scratch):
    odd, odd_lon = parities(axes)
    sems = scratch[-1]
    copies = [
        pltpu.make_async_copy(source, target, sems.at[n])
        for n, (source, target) in enumerate(
            zip((warm_hbm, signs_hbm, mask_hbm, kappa_hbm, scale_hbm), scratch[:-1], strict=True)
        )
    ]
    for copy in copies:
        copy.start()
    warm, signs, mask, kappa, scale = scratch[:-1]
    rows = [own.at[jnp.where(odd_lon == 0, p, ROWS - 1 - p)] for p in range(ROWS)]
    copies[0].wait()
    for p, row in enumerate(rows):
        row[0:PROBES, :] = warm[:, p, :]
    copies[1].wait()
    for p, row in enumerate(rows):
        row[PROBES : 2 * PROBES, :] = 2.0 * signs[:, p, :].astype(jnp.float32) - 1.0
    for copy in copies[2:]:
        copy.wait()
    wet = mask[...].astype(jnp.float32)
    diag = kappa[...] + 4.0
    scaled = scale[...]
    for p, row in enumerate(rows):
        row[2 * PROBES :, :] = jnp.concatenate(
            [wet[p : p + 1], diag[p : p + 1], scaled[p : p + 1], jnp.zeros((5, LANES), jnp.float32)], axis=0
        )
    block = lax.broadcasted_iota(jnp.int32, (FIELDS, LANES), 1) // DEPTH
    left_edge = jnp.zeros((FIELDS, LANES), jnp.float32)
    right_edge = jnp.zeros((FIELDS, LANES), jnp.float32)
    for i in range(ROWS):
        row = own[i]
        for f in range(3):
            fields[f, i : i + 1, :] = row[2 * PROBES + f : 2 * PROBES + f + 1]
        turned = pltpu.roll(row, DEPTH * i, 1) if i else row
        left_edge = jnp.where(block == i, turned, left_edge)
        right_edge = jnp.where(block == (i - 1) % ROWS, turned, right_edge)
    to_even[...] = jnp.where(odd == 0, right_edge, left_edge)
    to_odd[...] = jnp.where(odd == 0, left_edge, right_edge)


def sides(odd, even_side, odd_side):
    return jnp.where(odd == 0, odd_side, even_side), jnp.where(odd == 0, even_side, odd_side)


SEND_PROBES = DEPTH * PROBES
SEND_FIELDS = SEND_PROBES + (DEPTH - 2) * PROBES
SEND_CORNER = SEND_FIELDS + 3 * DEPTH
SEND_ROWS = SEND_CORNER + FIELDS


def send_kernel(axes, own, fields, from_odd, from_even, to_odd, to_even):
    odd_lat, _ = parities(axes)
    lane = lax.broadcasted_iota(jnp.int32, (FIELDS, LANES), 1)
    before, after = sides(odd_lat, from_even[...], from_odd[...])
    first = jnp.where(lane < 64, after, pltpu.roll(before, 72, 1))
    last = jnp.where(lane < 64, pltpu.roll(after, 64, 1), pltpu.roll(before, 8, 1))
    for target, corner, low, row in (
        (to_odd, first, 0, lambda j: j),
        (to_even, last, DEPTH, lambda j: ROWS - 1 - j),
    ):
        for j in range(DEPTH):
            target[j * PROBES : (j + 1) * PROBES, :] = own[row(j), 0:PROBES, :]
        for j in range(DEPTH - 2):
            target[SEND_PROBES + j * PROBES : SEND_PROBES + (j + 1) * PROBES, :] = own[row(j), PROBES : 2 * PROBES, :]
        for f in range(3):
            target[SEND_FIELDS + f * DEPTH : SEND_FIELDS + (f + 1) * DEPTH, :] = fields[f, low : low + DEPTH, :]
        target[SEND_CORNER:, :] = corner


TALL = ROWS + 2 * DEPTH
INSIDE = dict(mp=(8, 24), up=(9, 23), mw=(8, 24), i0=(9, 23), p0=(10, 22), m0=(10, 22), i1=(11, 21), p1=(12, 20), m1=(12, 20), i2=(13, 19), p2=(14, 18), m2=(14, 18), i3=(15, 17), p3=(16, 16))
NEEDED = dict(mp=(7, 25), up=(8, 24), mw=(0, 32), i0=(1, 31), p0=(2, 30), m0=(2, 30), i1=(3, 29), p1=(4, 28), m1=(4, 28), i2=(5, 27), p2=(6, 26), m2=(6, 26), i3=(7, 25), p3=(8, 24))
HELD = tuple(name for name in INSIDE if name != "p3")
HALF = ROWS // 2


def fill_coef(coef, at, wet, diag, scaled):
    coef[at, 0:1, :] = wet
    coef[at, 1:2, :] = diag
    coef[at, 2:3, :] = wet * scaled
    coef[at, 3:4, :] = GAIN * wet
    coef[at, 4:5, :] = GAIN * ((1.0 - wet) - SHIFT)


def march(rows, coef, warm, probe, get, put):
    def stencil(name, r):
        here = get(name, r)
        around = get(name, r - 1) + get(name, r + 1)
        around = around + (pltpu.roll(here, 1, 1) + pltpu.roll(here, 2 * LANES - 1, 1))
        return coef(r, 1) * here - around

    for r in rows("mp"):
        put("mp", r, coef(r, 0) * probe(r))
    for r in rows("mw"):
        put("mw", r, coef(r, 0) * warm(r))
    for r in rows("i0"):
        put("i0", r, coef(r, 2) * stencil("mw", r))
    for r in rows("up"):
        put("up", r, coef(r, 2) * stencil("mp", r))
    for k in range(4):
        power = f"p{k}"
        for r in rows(power):
            if k == 0:
                value = probe(r) - (coef(r, 0) * stencil("i0", r) + (1.0 - coef(r, 0)) * warm(r))
            else:
                value = coef(r, 3) * stencil(f"i{k}", r) + coef(r, 4) * get(f"p{k - 1}", r)
            put(power, r, value)
            if k < 3:
                put(f"m{k}", r, coef(r, 0) * value)
        for r in rows(f"i{k + 1}"):
            put(f"i{k + 1}", r, coef(r, 2) * stencil(f"m{k}", r))


def inside_kernel(axes, own, from_odd, from_even, wide, coefs, *held):
    odd_lat, _ = parities(axes)
    held = dict(zip(HELD, held, strict=True))
    lane = lax.broadcasted_iota(jnp.int32, (FIELDS, LANES), 1)
    before, after = sides(odd_lat, from_even[...], from_odd[...])
    for i in range(ROWS):
        turn = (LANES - 8 * i) % LANES
        wide[i, :, 0:LANES] = own[i]
        wide[i, :, LANES:] = jnp.where(lane < 64, pltpu.roll(after, turn, 1), pltpu.roll(before, turn, 1))
        fill_coef(coefs, i, wide[i, 64:65, :], wide[i, 65:66, :], wide[i, 66:67, :])

    def put(name, r, value):
        held[name][r - DEPTH] = value

    march(
        lambda name: range(*INSIDE.get(name, (0, 0))),
        lambda r, n: coefs[r - DEPTH, n : n + 1, :],
        lambda r: wide[r - DEPTH, 0:PROBES, :],
        lambda r: wide[r - DEPTH, PROBES : 2 * PROBES, :],
        lambda name, r: held[name][r - DEPTH],
        put,
    )


def half_kernel(behind, own_wide, own_coefs, *refs):
    held = dict(zip(HELD, refs, strict=False))
    refs = refs[len(HELD) :]
    if behind:
        other, message, sums, basis, images, probe_image, wide, coefs, *fresh = refs
    else:
        message, sums, basis, images, probe_image, wide, coefs, *fresh = refs
    fresh = dict(zip(NEEDED, fresh, strict=True))
    lane = lax.broadcasted_iota(jnp.int32, (FIELDS, LANES), 1)
    pair = message[SEND_CORNER:, :]
    for j in range(DEPTH):
        place = DEPTH - 1 - j if behind else j
        wide[j, 0:PROBES, 0:LANES] = message[j * PROBES : (j + 1) * PROBES, :]
        if j < DEPTH - 2:
            at = SEND_PROBES + j * PROBES
            wide[j, PROBES : 2 * PROBES, 0:LANES] = message[at : at + PROBES, :]
        for f in range(3):
            at = SEND_FIELDS + f * DEPTH + place
            wide[j, 2 * PROBES + f : 2 * PROBES + f + 1, 0:LANES] = message[at : at + 1, :]
        after = pltpu.roll(pair, (LANES - 8 * place) % LANES, 1)
        before = pltpu.roll(pair, (56 - 8 * place) % LANES, 1)
        wide[j, :, LANES:] = jnp.where(lane < 64, after, before)
        fill_coef(coefs, j, wide[j, 64:65, :], wide[j, 65:66, :], wide[j, 66:67, :])

    base = TALL // 2 if behind else 0

    def own(r):
        return DEPTH <= r < DEPTH + ROWS

    def halo(r):
        return r - (DEPTH + ROWS) if behind else DEPTH - 1 - r

    def rows(name):
        if name not in NEEDED:
            return range(0)
        return range(INSIDE[name][1], NEEDED[name][1]) if behind else range(NEEDED[name][0], INSIDE[name][0])

    def get(name, r, lanes=2 * LANES):
        return fresh[name][r - base, :, 0:lanes] if r in rows(name) else held[name][r - DEPTH, :, 0:lanes]

    def put(name, r, value):
        if name in ("p3", "up"):
            fresh[name][r - base, :, 0:LANES] = value[:, 0:LANES]
        else:
            fresh[name][r - base] = value

    def coef(r, n):
        return own_coefs[r - DEPTH, n : n + 1, :] if own(r) else coefs[halo(r), n : n + 1, :]

    def argument(r, at):
        return own_wide[r - DEPTH, at : at + PROBES, :] if own(r) else wide[halo(r), at : at + PROBES, :]

    march(rows, coef, lambda r: argument(r, 0), lambda r: argument(r, PROBES), get, put)

    total = other[...] if behind else jnp.zeros((3 * PROBES, 4 * PROBES), jnp.float32)
    for i in range(HALF):
        r = DEPTH + i + (HALF if behind else 0)
        for k in range(4):
            at = slice(k * PROBES, (k + 1) * PROBES)
            basis[i, at, :] = get(f"p{k}", r, LANES)
            images[i, at, :] = get(f"i{(k + 1) % 4}", r, LANES)
        probe_image[i] = get("up", r, LANES)
        if i % 2 == 0:
            continue
        block = jnp.concatenate([basis[i - 1], basis[i]], axis=1)
        total = total + lax.dot_general(
            block[0 : 3 * PROBES],
            block,
            (((1,), (1,)), ((), ())),
            precision=lax.Precision.HIGHEST,
            preferred_element_type=jnp.float32,
        )
    if not behind:
        sums[...] = total
        return
    lane = lax.broadcasted_iota(jnp.int32, (PROBES, LANES), 1)
    row = lax.broadcasted_iota(jnp.int32, (PROBES, LANES), 0)
    packed = jnp.zeros((PROBES, LANES), jnp.float32)
    for b in range(3):
        even = total[b * PROBES : (b + 1) * PROBES]
        odd = pltpu.roll(even, LANES - PROBES, 1)
        column = lane - b * PROBES
        inside = (column >= 0) & (column < PROBES)
        packed = jnp.where(inside, jnp.where(column >= row, even, odd), packed)
        odd_diagonal = jnp.sum(jnp.where(column == row, odd, 0.0), axis=1, keepdims=True)
        packed = jnp.where(lane == 3 * PROBES + b, odd_diagonal, packed)
    sums[...] = packed


def dot(left, right, precision):
    return jnp.dot(left, right, precision=precision, preferred_element_type=jnp.float32)


def invert_pair(p):
    scale = 1.0 / (p[0][0] * p[1][1] - p[0][1] * p[0][1])
    return p[1][1] * scale, -p[0][1] * scale, p[0][0] * scale


def prepare(p):
    n = len(p)
    if n == 2:
        a, b, c = invert_pair(p)
        return lambda r: [a * r[0] + b * r[1], b * r[0] + c * r[1]]
    h = n // 2
    top = prepare([row[:h] for row in p[:h]])
    side = [row[h:] for row in p[:h]]
    solved = list(zip(*[top([side[i][j] for i in range(h)]) for j in range(h)], strict=True))

    def product(rows, weights):
        terms = [row * weight for row, weight in zip(rows, weights, strict=True)]
        while len(terms) > 1:
            terms = [sum(terms[i : i + 2][1:], terms[i]) for i in range(0, len(terms), 2)]
        return terms[0]

    rest = [[None] * h for _ in range(h)]
    for i in range(h):
        for j in range(i, h):
            rest[i][j] = p[h + i][h + j] - product([side[t][i] for t in range(h)], [solved[t][j] for t in range(h)])
            rest[j][i] = rest[i][j]
    bottom = prepare(rest)

    def solve(r):
        upper = top(r[:h])
        lower = bottom([r[h + i] - product([side[t][i] for t in range(h)], upper) for i in range(h)])
        return [upper[t] - product(solved[t], lower) for t in range(h)] + lower

    return solve


def eliminate(parts):
    row = lax.broadcasted_iota(jnp.int32, (8, LANES), 0)

    def spread(value):
        return jnp.broadcast_to(value, (8, LANES))

    def take(part, lane):
        return jnp.take_along_axis(part, jnp.full((8, LANES), lane, jnp.int32), axis=1)

    for home in range(len(parts)):
        at = 8 * home
        column = [take(parts[home], at + j) for j in range(8)]
        pivot = [[spread(column[j][i : i + 1]) for j in range(8)] for i in range(8)]
        solved = prepare(pivot)([spread(parts[home][i : i + 1]) for i in range(8)])
        for v in [*range(home, len(parts)), *range(home)]:
            if v == home:
                part = solved[0]
                for i in range(1, 8):
                    part = jnp.where(row == i, solved[i], part)
                parts[v] = part
            else:
                terms = [take(parts[v], at + j) * solved[j] for j in range(8)]
                parts[v] = parts[v] - (
                    ((terms[0] + terms[1]) + (terms[2] + terms[3])) + ((terms[4] + terms[5]) + (terms[6] + terms[7]))
                )
    return parts


def finish_kernel(
    axes,
    sums, own, basis_first, basis_last, images_first, images_last, probe_first, probe_last,
    solution_out, residual_out, grad_out,
    coeffs,
):
    _, odd_lon = parities(axes)
    packed = sums[...]
    flipped = packed.T
    lane = lax.broadcasted_iota(jnp.int32, (PROBES, PROBES), 1)
    row = lax.broadcasted_iota(jnp.int32, (PROBES, PROBES), 0)
    moments = []
    for b in range(3):
        block = packed[:, b * PROBES : (b + 1) * PROBES]
        mirror = flipped[b * PROBES : (b + 1) * PROBES, :]
        moments.append(jnp.where(lane >= row, block, mirror))
        odd = jnp.where(lane < row, block, mirror)
        moments.append(jnp.where(lane == row, packed[:, 3 * PROBES + b : 3 * PROBES + b + 1], odd))
    power = [moments[k + 1] * (1.0 / GAIN) + moments[k] * SHIFT for k in range(5)]

    table = jnp.concatenate(
        [jnp.concatenate([power[b], power[b + 1], power[b + 2], moments[b]], axis=1) for b in range(3)], axis=0
    )
    parts = eliminate([table[8 * v : 8 * v + 8] for v in range(12)])
    solved = jnp.concatenate(parts, axis=0)

    t = [jnp.sum(jnp.where(lane == row, m, 0.0), axis=(0, 1), keepdims=True) for m in moments]
    a = t[1] / t[0]
    n1 = t[2] - a * t[1]
    b0, b1 = (t[2] / t[0], (t[3] - a * t[2]) / n1)
    b2 = b1 * a - b0
    c0, c1 = (t[3] / t[0], (t[4] - a * t[3]) / n1)
    c2 = (t[5] - b1 * t[4] + b2 * t[3]) / (t[4] - b1 * t[3] + b2 * t[2])

    nothing = jnp.zeros((PROBES, LANES), jnp.float32)
    wide_lane = lax.broadcasted_iota(jnp.int32, (4 * PROBES, LANES), 1)
    wide_row = lax.broadcasted_iota(jnp.int32, (4 * PROBES, LANES), 0)
    one = (wide_lane == wide_row + 3 * PROBES).astype(jnp.float32)
    kept = jnp.concatenate([solved, nothing], axis=0)
    left = one - SHIFT * kept - (1.0 / GAIN) * jnp.concatenate([nothing, solved], axis=0)

    def for_polynomials(v):
        v = [v[k * PROBES : (k + 1) * PROBES] for k in range(4)]
        return jnp.concatenate(
            [v[0] + a * v[1] + b0 * v[2] + c0 * v[3], v[1] + b1 * v[2] + c1 * v[3], v[2] + c2 * v[3], v[3]], axis=0
        )

    columns = jnp.where(
        wide_lane < PROBES,
        pltpu.roll(for_polynomials(kept), PROBES, 1),
        jnp.where(wide_lane < 2 * PROBES, pltpu.roll(for_polynomials(left), 2 * PROBES, 1), pltpu.roll(kept, 3 * PROBES, 1)),
    )
    coeffs[...] = columns.T[0 : 3 * PROBES]
    weights = coeffs[2 * PROBES :, :] + one[0:PROBES]
    a, b0, b1, c0, c1, c2 = (jnp.broadcast_to(x, (PROBES, LANES)) for x in (a, b0, b1, c0, c1, c2))

    for i in range(0, ROWS, 2):
        j = i % HALF
        basis, images, probe_image = (
            (basis_first, images_first, probe_first) if i < HALF else (basis_last, images_last, probe_last)
        )
        polynomials = []
        for n in (j, j + 1):
            v0 = basis[n, 0:PROBES, :]
            w1 = basis[n, PROBES : 2 * PROBES, :] - a * v0
            w2 = basis[n, 2 * PROBES : 3 * PROBES, :] - b1 * w1 - b0 * v0
            w3 = basis[n, 3 * PROBES :, :] - c2 * w2 - c1 * w1 - c0 * v0
            polynomials.append(jnp.concatenate([v0, w1, w2, w3], axis=0))
        both = dot(coeffs[0 : 2 * PROBES, :], jnp.concatenate(polynomials, axis=1), lax.Precision.HIGH)
        image = dot(weights, jnp.concatenate([images[j], images[j + 1]], axis=1), lax.Precision.HIGH)
        for n in range(2):
            lanes = slice(n * LANES, (n + 1) * LANES)
            values = both[0:PROBES, lanes] + own[i + n, 0:PROBES, :]
            terms = values * probe_image[j + n] + image[:, lanes] * own[i + n, PROBES : 2 * PROBES, :]
            wet = own[i + n, 64:65, :]
            place = jnp.where(odd_lon == 0, i + n, ROWS - 1 - i - n)
            solution_out[:, pl.ds(place, 1), :] = values.reshape(PROBES, 1, LANES)
            residual_out[:, pl.ds(place, 1), :] = both[PROBES:, lanes].reshape(PROBES, 1, LANES)
            grad_out[pl.ds(place, 1), :] = wet * (jnp.sum(terms, axis=0, keepdims=True) * (1.0 / PROBES))


def f32(*shape):
    return jax.ShapeDtypeStruct(shape, jnp.float32)


def exchanged(value, axes, odd, wrap):
    size = lax.axis_size(axes)
    pairs = []
    for i in range(size):
        other = ((i + odd) ^ 1) - odd
        if wrap or 0 <= other < size:
            pairs.append((i, other % size))
    return lax.ppermute(value, axes, pairs)


def spread_sum(value, axes):
    size = lax.axis_size(axes)
    copies = jnp.broadcast_to(value[None], (size,) + value.shape)
    return jnp.sum(lax.all_to_all(copies, axes, 0, 0), axis=0)


def make_local(lat, lon, stages):
    axes = (lat[-1], lon[-1])

    def local(warm_start, probe_signs, ocean_mask, kappa_sq, scale_field):
        args = (warm_start, probe_signs, ocean_mask, kappa_sq, scale_field)
        own, fields, to_odd, to_even = pl.pallas_call(
            functools.partial(pack_kernel, axes),
            out_shape=(
                f32(ROWS, FIELDS, LANES),
                f32(3, ROWS, LANES),
                f32(FIELDS, LANES),
                f32(FIELDS, LANES),
            ),
            in_specs=[pl.BlockSpec(memory_space=pltpu.HBM)] * 5,
            scratch_shapes=[pltpu.VMEM(x.shape, x.dtype) for x in args] + [pltpu.SemaphoreType.DMA((5,))],
            compiler_params=PARAMS,
            name="pack_edges",
        )(*(pltpu.with_memory_space_constraint(x, pltpu.HBM) for x in args))
        odd_lat = exchanged(to_odd, lat, 1, False)
        even_lat = exchanged(to_even, lat, 0, False)
        to_odd, to_even = pl.pallas_call(
            functools.partial(send_kernel, axes),
            out_shape=(f32(SEND_ROWS, LANES), f32(SEND_ROWS, LANES)),
            compiler_params=PARAMS,
            name="pack_rows",
        )(own, fields, odd_lat, even_lat)
        odd_lon = exchanged(to_odd, lon, 1, True)
        even_lon = exchanged(to_even, lon, 0, True)
        inside = pl.pallas_call(
            functools.partial(inside_kernel, axes),
            out_shape=(f32(ROWS, FIELDS, 2 * LANES), f32(ROWS, 8, 2 * LANES))
            + (f32(ROWS, PROBES, 2 * LANES),) * len(HELD),
            compiler_params=PARAMS,
            cost_estimate=pl.CostEstimate(flops=40_000_000, bytes_accessed=8_000_000, transcendentals=0),
            name="inside_rows",
        )(own, odd_lat, even_lat)
        half = dict(
            scratch_shapes=[
                pltpu.VMEM((DEPTH, FIELDS, 2 * LANES), jnp.float32),
                pltpu.VMEM((DEPTH, 8, 2 * LANES), jnp.float32),
            ]
            + [pltpu.VMEM((TALL // 2, PROBES, 2 * LANES), jnp.float32)] * len(NEEDED),
            compiler_params=PARAMS,
            cost_estimate=pl.CostEstimate(flops=40_000_000, bytes_accessed=8_000_000, transcendentals=0),
        )
        filled = (f32(HALF, 4 * PROBES, LANES), f32(HALF, 4 * PROBES, LANES), f32(HALF, PROBES, LANES))
        part, *first = pl.pallas_call(
            functools.partial(half_kernel, False),
            out_shape=(f32(3 * PROBES, LANES), *filled),
            name="first_rows",
            **half,
        )(*inside, odd_lon)
        sums, *last = pl.pallas_call(
            functools.partial(half_kernel, True),
            out_shape=(f32(PROBES, LANES), *filled),
            name="last_rows",
            **half,
        )(*inside, part, even_lon)
        with jax.named_scope("sum_moments"):
            for group in stages:
                sums = spread_sum(sums, group)
        return pl.pallas_call(
            functools.partial(finish_kernel, axes),
            out_shape=(
                f32(PROBES, ROWS, LANES),
                f32(PROBES, ROWS, LANES),
                f32(ROWS, LANES),
            ),
            scratch_shapes=[
                pltpu.VMEM((3 * PROBES, 4 * PROBES), jnp.float32),
            ],
            compiler_params=PARAMS,
            name="solve_and_combine",
        )(sums, own, *(x for pair in zip(first, last, strict=True) for x in pair))

    return local


def solution(mesh):
    if mesh.devices.shape == (16, 32):
        grid = Mesh(mesh.devices.reshape(2, 4, 2, 4, 8), ("zh", "x", "c", "zl", "y"))
        lat, lon = (("zh", "x", "c"), ("zl", "y"))
        stages = (("x", "c"), ("zh", "zl"), ("y",))
    else:
        grid, lat, lon, stages = (mesh, ("lat",), ("lon",), (("lat",), ("lon",)))
    return jax.shard_map(
        make_local(lat, lon, stages),
        mesh=grid,
        in_specs=(P(None, lon, lat), P(None, lon, lat), P(lon, lat), P(lon, lat), P(lon, lat)),
        out_specs=(P(None, lon, lat), P(None, lon, lat), P(lon, lat)),
        check_vma=False,
    )
```
